32 devices in a mesh: ctx: 16 (over z, y, core), ch: 2 (over x).
Axes of the slice: x: 2, y: 2, z: 4, core: 2. Of those that a mesh axis runs over, the one named last changes fastest.
Arguments:
- mamba_input: bfloat16 [1024, 16384], P(('ctx', 'ch')), may hold values from -6 to 6
- mamba_gate: bfloat16 [1024, 16384], P(('ctx', 'ch')), may hold values from -6 to 6
- conv_weight: float32 [4, 16384], P(None, 'ch'), may hold values from -3 to 3
- conv_bias: float32 [16384], P('ch'), may hold values from -3 to 3
- step_down: bfloat16 [16384, 512], P('ch'), may hold values from -0.046875 to 0.046875
- state_proj: bfloat16 [16384, 32], P('ch'), may hold values from -0.046875 to 0.046875
- step_up: bfloat16 [512, 16384], P(None, 'ch'), may hold values from -0.0625 to 0.0625
- step_bias: float32 [16384], P('ch'), may hold values from -5 to -4
- decay_rate: float32 [16, 16384], P(None, 'ch'), may hold values from 0 to 3, as said below
- skip_gain: float32 [16384], P('ch'), may hold values from 0.5 to 1.5
- queries: bfloat16 [1024, 8192], P('ctx', 'ch'), may hold values from -6 to 6
- key_rows: bfloat16 [1024, 1024], P('ctx', 'ch'), may hold values from -6 to 6
- value_rows: bfloat16 [1024, 1024], P('ctx', 'ch'), may hold values from -6 to 6
Outputs:
- mamba_out: bfloat16 [1024, 16384], P(('ctx', 'ch'))
- attention_out: bfloat16 [1024, 8192], P('ctx', 'ch')
The draws below stay inside these ranges and needn't reach their ends.
Inputs may be any that keep to these rules, and one draw needn't show every extreme that they name: `decay_rate`: positive decay rates.
All inputs are finite; a program needn't handle non-finite values.
Results may differ from the reference program's by a relative error of at most 0.013.
Values may be sent and summed in bfloat16 or wider, within the bound.
A program may use at most 320 MiB of HBM per device.

```python
import math
import jax
import jax.numpy as jnp
from jax import lax

INNER = 16384
STATE = 16
CONV = 4
STEP_RANK = 512
HEADS = 64
KV_HEADS = 8
HEAD_DIM = 128
SEQ = 1024


def draw_decay_rate(key, part):
    pick_key, slow_key, fast_key = jax.random.split(key, 3)
    slow_share = 0.5
    slow_side = jax.random.uniform(pick_key, (1, INNER), jnp.float32) < slow_share
    slow_rate = 100.0 / SEQ * jnp.exp(jax.random.uniform(slow_key, (STATE, INNER), jnp.float32, math.log(0.1), 0.0))
    fast_rate = jnp.exp(jax.random.uniform(fast_key, (STATE, INNER), jnp.float32, 0.0, math.log(3.0)))
    return jnp.where(slow_side, slow_rate, fast_rate).astype(jnp.float32)


def draw_key_rows(key, part):
    drawn = jnp.clip(jax.random.normal(jax.random.fold_in(key, 1), (SEQ, KV_HEADS * HEAD_DIM), jnp.float32), -6.0, 6.0)
    return drawn.astype(jnp.bfloat16)


def draw_queries(key, part):
    drawn = jnp.clip(jax.random.normal(jax.random.fold_in(key, 2), (SEQ, HEADS * HEAD_DIM), jnp.float32), -6.0, 6.0)
    return drawn.astype(jnp.bfloat16)


def levels(rng, dims, cuts, least, top_value):
    def one(axis_at, shards_of):
        steps = jax.random.uniform(jax.random.fold_in(jax.random.fold_in(rng, 6), axis_at), (shards_of,), jnp.float32, least / len(cuts), top_value / len(cuts))
        return jnp.repeat(jnp.exp(steps), dims[axis_at] // shards_of).reshape((-1,) + (1,) * (len(dims) - axis_at - 1))

    level = one(*cuts[0])
    for cut in cuts[1:]:
        level = level * one(*cut)
    return level


def scatter_about(own_key, shape, spread, bound, shards=(), held_as=jnp.bfloat16):
    values = spread * jax.random.normal(own_key, shape, jnp.float32)
    if shards:
        values = values * levels(own_key, shape, shards, -0.22, 0.18)
    return jnp.clip(values, -bound, bound).astype(held_as)


def setup_inputs(seed: int = 0) -> dict:
    arg_keys = jax.random.split(jax.random.key(seed), 14)
    mamba_input = scatter_about(arg_keys[0], (SEQ, INNER), 1.0, 6.0, ((0, 32),))
    mamba_gate = scatter_about(arg_keys[1], (SEQ, INNER), 1.0, 6.0, ((0, 32),))
    conv_weight = scatter_about(arg_keys[2], (CONV, INNER), CONV ** -0.5, 3.0, ((1, 2),), jnp.float32)
    conv_bias = scatter_about(arg_keys[3], (INNER,), 0.5, 3.0, ((0, 2),), jnp.float32)
    step_down = scatter_about(arg_keys[4], (INNER, STEP_RANK), INNER ** -0.5, 0.046875, ((0, 2),))
    state_proj = scatter_about(arg_keys[5], (INNER, 2 * STATE), INNER ** -0.5, 0.046875, ((0, 2),))
    step_up = scatter_about(arg_keys[6], (STEP_RANK, INNER), (STEP_RANK * 16) ** -0.5, 0.0625, ((1, 2),))
    step_bias = jnp.clip(-5.0 + 1.0 * jax.random.uniform(arg_keys[7], (INNER,), jnp.float32) ** levels(arg_keys[7], (INNER,), ((0, 2),), -0.2, 0.2), -5.0, -4.0)
    decay_rate = draw_decay_rate(jax.random.fold_in(arg_keys[13], 71), 0)
    skip_gain = jnp.clip(0.5 + 1.0 * jax.random.uniform(arg_keys[9], (INNER,), jnp.float32) ** levels(arg_keys[9], (INNER,), ((0, 2),), -0.2, 0.2), 0.5, 1.5)
    queries = draw_queries(jax.random.fold_in(arg_keys[13], 71), 0)
    key_rows = draw_key_rows(jax.random.fold_in(arg_keys[13], 71), 0)
    value_rows = scatter_about(arg_keys[12], (SEQ, KV_HEADS * HEAD_DIM), 1.0, 6.0, ((0, 16), (1, 2)))
    return dict(mamba_input=mamba_input, mamba_gate=mamba_gate, conv_weight=conv_weight, conv_bias=conv_bias, step_down=step_down, state_proj=state_proj, step_up=step_up, step_bias=step_bias, decay_rate=decay_rate, skip_gain=skip_gain, queries=queries, key_rows=key_rows, value_rows=value_rows)


def mamba_part(mamba_input, mamba_gate, conv_weight, conv_bias, step_down, state_proj, step_up, step_bias, decay_rate, skip_gain):
    inputs_f = mamba_input.astype(jnp.float32)
    padded = jnp.concatenate([jnp.zeros((CONV - 1, INNER), jnp.float32), inputs_f], axis=0)
    conv_sum = conv_bias[None, :] + sum((conv_weight[tap_index][None, :] * padded[tap_index:tap_index + SEQ] for tap_index in range(CONV)))
    activation = jax.nn.silu(conv_sum).astype(jnp.bfloat16)
    step_low = jnp.dot(activation, step_down, preferred_element_type=jnp.float32).astype(jnp.bfloat16)
    state_terms = jnp.dot(activation, state_proj, preferred_element_type=jnp.float32)
    step_size = jax.nn.softplus(jnp.dot(step_low, step_up, preferred_element_type=jnp.float32) + step_bias[None, :])
    activation_f = activation.astype(jnp.float32)

    def advance(carried, token_inputs):
        step_row, act_row, terms_row = token_inputs
        input_mix = terms_row[:STATE]
        output_mix = terms_row[STATE:]
        carried = jnp.exp(-decay_rate * step_row[None, :]) * carried + (step_row * act_row)[None, :] * input_mix[:, None]
        return (carried, lax.optimization_barrier(jnp.sum(output_mix[:, None] * carried, axis=0)))
    final_state, scanned = lax.scan(advance, jnp.zeros((STATE, INNER), jnp.float32), (step_size, activation_f, state_terms))
    scan_out = (scanned + skip_gain[None, :] * activation_f).astype(jnp.bfloat16)
    scan_out = lax.optimization_barrier(scan_out)
    return (scan_out.astype(jnp.float32) * jax.nn.silu(mamba_gate.astype(jnp.float32))).astype(jnp.bfloat16)

def attention_part(queries, key_rows, value_rows):
    group_size = HEADS // KV_HEADS
    scale_factor = 1.0 / math.sqrt(HEAD_DIM)
    block_len = math.gcd(SEQ, 512)
    query_blocks = queries.reshape(SEQ // block_len, block_len, HEADS, HEAD_DIM)
    key_heads = key_rows.reshape(SEQ, KV_HEADS, HEAD_DIM)
    value_heads = value_rows.reshape(SEQ, KV_HEADS, HEAD_DIM)
    positions = jnp.arange(SEQ, dtype=jnp.int32)

    def one_block(block_inputs):
        query_block, first_row = block_inputs
        query_pos = first_row + jnp.arange(block_len, dtype=jnp.int32)
        visible = positions[None, :] <= query_pos[:, None]

        def one_head(head_index):
            group_index = head_index // group_size
            keys_here = lax.dynamic_index_in_dim(key_heads, group_index, 1, keepdims=False)
            values_here = lax.dynamic_index_in_dim(value_heads, group_index, 1, keepdims=False)
            query_here = lax.dynamic_index_in_dim(query_block, head_index, 1, keepdims=False)
            scores = jnp.dot(query_here, keys_here.T, preferred_element_type=jnp.float32) * scale_factor
            masked = jnp.where(visible, scores, -1e+30)
            top_score = lax.optimization_barrier(jnp.max(masked, axis=1, keepdims=True))
            weights = jnp.where(visible, jnp.exp(masked - top_score), 0.0)
            total = lax.optimization_barrier(jnp.sum(weights, axis=1, keepdims=True))
            return jnp.dot(weights.astype(jnp.bfloat16), values_here, preferred_element_type=jnp.float32) / total
        per_head = lax.map(one_head, jnp.arange(HEADS, dtype=jnp.int32))
        return per_head.transpose(1, 0, 2).reshape(block_len, HEADS * HEAD_DIM).astype(jnp.bfloat16)
    block_starts = jnp.arange(SEQ // block_len, dtype=jnp.int32) * block_len
    result = lax.map(one_block, (query_blocks, block_starts))
    return result.reshape(SEQ, HEADS * HEAD_DIM)

def reference(mamba_input, mamba_gate, conv_weight, conv_bias, step_down, state_proj, step_up, step_bias, decay_rate, skip_gain, queries, key_rows, value_rows):
    mamba_out = mamba_part(mamba_input, mamba_gate, conv_weight, conv_bias, step_down, state_proj, step_up, step_bias, decay_rate, skip_gain)
    attention_out = attention_part(queries, key_rows, value_rows)
    return (mamba_out, attention_out)
```

```python
import functools
import math

import jax
import jax.numpy as jnp
from jax import lax
from jax.experimental import pallas as pl
from jax.experimental.pallas import tpu as pltpu
from jax.sharding import PartitionSpec as P

STATE = 16
CONV = 4
HEADS = 64
KV_HEADS = 8
HEAD_DIM = 128


def passed_along(array, axis, by):
    size = lax.axis_size(axis)
    pairs = [(i, i + by) for i in range(size) if 0 <= i + by < size]
    return lax.ppermute(array, axis, pairs)


LANES = 128
SUBS = 8
TILE = LANES * SUBS
LOG2E = math.log2(math.e)
MESH = pl.DeviceIdType.MESH


def to_rows(dst_ref, value):
    rows = value.shape[0]
    for sub in range(SUBS):
        dst_ref[pl.ds(sub, rows, stride=SUBS), :] = value[:, sub * LANES : (sub + 1) * LANES]


def spread_terms(terms_ref, spread_ref, count):
    rows = terms_ref.shape[0]
    for n in range(count):
        spread_ref[n * rows : (n + 1) * rows, :] = jnp.broadcast_to(
            terms_ref[:, n : n + 1], (rows, LANES)
        )


def row_of(spread_ref, index):
    return spread_ref[pl.ds(index, SUBS, stride=0), :]


def first_pass(low_ref, up_ref, bias_ref, act_ref, terms_ref, decay_ref,
               step_ref, end_ref, total_ref, spread, act_rows, rates):
    rows = act_ref.shape[0]

    @pl.when(pl.program_id(0) == 0)
    def _():
        spread_terms(terms_ref, spread, STATE)

    pre = jnp.dot(low_ref[...], up_ref[...], preferred_element_type=jnp.float32) + bias_ref[...]
    to_rows(step_ref.at[0], jax.nn.softplus(pre))
    to_rows(act_rows, act_ref[...].astype(jnp.float32))
    to_rows(rates, decay_ref[...] * (-LOG2E))
    rate = [rates[n * SUBS : (n + 1) * SUBS, :] for n in range(STATE)]

    def token(t, carry):
        states, total = carry
        at = pl.multiple_of(t * SUBS, SUBS)
        step = step_ref[0, pl.ds(at, SUBS), :]
        push = step * act_rows[pl.ds(at, SUBS), :]
        states = tuple(
            jnp.exp2(step * rate[n]) * states[n] + push * row_of(spread, n * rows + t)
            for n in range(STATE)
        )
        return states, total + step

    zero = jnp.zeros((SUBS, LANES), jnp.float32)
    states, total = lax.fori_loop(0, rows, token, ((zero,) * STATE, zero), unroll=4)
    for n in range(STATE):
        end_ref[0, n] = states[n]
    total_ref[0] = total


def second_pass(step_ref, act_ref, terms_ref, decay_ref, incoming_ref, gate_ref, skip_ref,
                out_ref, spread, act_rows, rates, outs):
    rows = act_ref.shape[0]

    @pl.when(pl.program_id(0) == 0)
    def _():
        spread_terms(terms_ref, spread, 2 * STATE)

    to_rows(act_rows, act_ref[...].astype(jnp.float32))
    to_rows(rates, decay_ref[...] * (-LOG2E))
    rate = [rates[n * SUBS : (n + 1) * SUBS, :] for n in range(STATE)]

    def token(t, states):
        at = pl.multiple_of(t * SUBS, SUBS)
        step = step_ref[0, pl.ds(at, SUBS), :]
        push = step * act_rows[pl.ds(at, SUBS), :]
        new, parts = [], []
        for n in range(STATE):
            state = jnp.exp2(step * rate[n]) * states[n] + push * row_of(spread, n * rows + t)
            new.append(state)
            term = state * row_of(spread, (STATE + n) * rows + t)
            if n < 2:
                parts.append(term)
            else:
                parts[n % 2] = parts[n % 2] + term
        outs[pl.ds(at, SUBS), :] = parts[0] + parts[1]
        return tuple(new)

    lax.fori_loop(0, rows, token, tuple(incoming_ref[0, n] for n in range(STATE)), unroll=4)
    for sub in range(SUBS):
        cols = slice(sub * LANES, (sub + 1) * LANES)
        mixed = outs[pl.ds(sub, rows, stride=SUBS), :]
        mixed = mixed + skip_ref[:, cols] * act_ref[:, cols].astype(jnp.float32)
        mixed = mixed.astype(jnp.bfloat16).astype(jnp.float32)
        out_ref[:, cols] = (mixed * jax.nn.silu(gate_ref[:, cols].astype(jnp.float32))).astype(
            jnp.bfloat16
        )


def exchange(n_ctx, rows_state, rows_total, send_ref, rate_ref, back_ref,
             got, reply, send_sem, got_sem, reply_sem, back_sem):
    me = lax.axis_index("ctx")
    barrier = pltpu.get_barrier_semaphore()
    for k in range(1, n_ctx):
        peer = lax.rem(me + k, n_ctx)
        pl.semaphore_signal(barrier, inc=1, device_id={"ctx": peer}, device_id_type=MESH)
    pl.semaphore_wait(barrier, n_ctx - 1)

    def there(k):
        peer = lax.rem(me + k, n_ctx)
        return pltpu.make_async_remote_copy(
            src_ref=send_ref.at[peer], dst_ref=got.at[me], send_sem=send_sem.at[k],
            recv_sem=got_sem.at[k], device_id={"ctx": peer}, device_id_type=MESH)

    def back(k):
        peer = lax.rem(me + k, n_ctx)
        return pltpu.make_async_remote_copy(
            src_ref=reply.at[peer], dst_ref=back_ref.at[me], send_sem=reply_sem.at[k],
            recv_sem=back_sem.at[k], device_id={"ctx": peer}, device_id_type=MESH)

    for k in range(1, n_ctx):
        there(k).start()
    got[me] = send_ref[me]
    for k in range(1, n_ctx):
        there(k).wait()

    state_shape = (rows_state, LANES)
    reps = rows_state // rows_total

    def combine(i, carry):
        sent = carry
        if reply.shape[1] > rows_state:
            spare = jnp.zeros((reply.shape[1] - rows_state, LANES), jnp.float32)
            sent = jnp.concatenate([carry, spare], axis=0)
        reply[i] = sent.astype(jnp.bfloat16)
        block = got[i].astype(jnp.float32)
        total = (block[rows_state : rows_state + rows_total]
                 + block[rows_state + rows_total : rows_state + 2 * rows_total])
        wide = jnp.concatenate([total] * reps, axis=0)
        return jnp.exp2(rate_ref[...] * wide) * carry + block[:rows_state]

    lax.fori_loop(0, n_ctx, combine, jnp.zeros(state_shape, jnp.float32))
    for k in range(1, n_ctx):
        back(k).start()
    back_ref[me] = reply[me]
    for k in range(1, n_ctx):
        back(k).wait()


def attend(queries, key_rows, value_rows):
    rows_here = queries.shape[0]
    groups_here = key_rows.shape[1] // HEAD_DIM
    group_size = HEADS // KV_HEADS
    scale_factor = 1.0 / math.sqrt(HEAD_DIM)
    query_heads = queries.reshape(rows_here, groups_here, group_size, HEAD_DIM)
    query_first = lax.axis_index("ctx") * rows_here
    query_pos = query_first + jnp.arange(rows_here, dtype=jnp.int32)
    initial = (
        jnp.full((groups_here, group_size, rows_here), -1e30, jnp.float32),
        jnp.zeros((groups_here, group_size, rows_here), jnp.float32),
        jnp.zeros((groups_here, group_size, rows_here, HEAD_DIM), jnp.float32),
    )
    key_piece = lax.all_gather(key_rows, "ctx", axis=0, tiled=True)
    value_piece = lax.all_gather(value_rows, "ctx", axis=0, tiled=True)
    piece_rows = key_piece.shape[0]
    block_len = math.gcd(piece_rows, 512)

    def fold_one_block(block_index, inner_state):
        block_first = block_index * block_len
        key_block = lax.dynamic_slice_in_dim(
            key_piece, block_index * block_len, block_len, 0
        ).reshape(block_len, groups_here, HEAD_DIM)
        value_block = lax.dynamic_slice_in_dim(
            value_piece, block_index * block_len, block_len, 0
        ).reshape(block_len, groups_here, HEAD_DIM)

        def visit(visit_state):
            running_max, running_total, running_sum = visit_state
            scores = (
                jnp.einsum(
                    "tkgd,skd->kgts", query_heads, key_block, preferred_element_type=jnp.float32
                )
                * scale_factor
            )
            visible = (block_first + jnp.arange(block_len, dtype=jnp.int32))[None, :] <= query_pos[
                :, None
            ]
            masked = jnp.where(visible, scores, -1e30)
            new_max = jnp.maximum(running_max, jnp.max(masked, axis=3))
            weights = jnp.where(visible, jnp.exp(masked - new_max[..., None]), 0.0)
            rescale = jnp.exp(running_max - new_max)
            new_total = running_total * rescale + jnp.sum(weights, axis=3)
            new_sum = running_sum * rescale[..., None] + jnp.einsum(
                "kgts,skd->kgtd",
                weights.astype(jnp.bfloat16),
                value_block,
                preferred_element_type=jnp.float32,
            )
            return (new_max, new_total, new_sum)

        return lax.cond(
            block_first > query_first + rows_here - 1, lambda skipped: skipped, visit, inner_state
        )

    final_max, final_total, final_sum = lax.fori_loop(
        0, piece_rows // block_len, fold_one_block, initial
    )
    mixed = final_sum / final_total[..., None]
    return (
        mixed.transpose(2, 0, 1, 3)
        .reshape(rows_here, groups_here * group_size * HEAD_DIM)
        .astype(jnp.bfloat16)
    )


def local(
    mamba_input, mamba_gate, conv_weight, conv_bias, step_down, state_proj, step_up, step_bias,
    decay_rate, skip_gain, queries, key_rows, value_rows,
):
    n_ctx, n_ch = lax.axis_size("ctx"), lax.axis_size("ch")
    inner_in = lax.all_to_all(mamba_input, "ch", split_axis=1, concat_axis=0, tiled=True)
    inner_gate = lax.all_to_all(mamba_gate, "ch", split_axis=1, concat_axis=0, tiled=True)
    rows, channels = inner_in.shape
    rim_rows = passed_along(inner_in[rows - (CONV - 1) :], "ctx", 1)
    padded = jnp.concatenate([rim_rows, inner_in], axis=0).astype(jnp.float32)
    conv_sum = conv_bias[None, :] + sum(
        conv_weight[tap][None, :] * padded[tap : tap + rows] for tap in range(CONV)
    )
    activation = jax.nn.silu(conv_sum).astype(jnp.bfloat16)
    low_part = jnp.dot(activation, step_down, preferred_element_type=jnp.float32)
    term_part = jnp.dot(activation, state_proj, preferred_element_type=jnp.float32)
    part = jnp.concatenate([low_part, term_part], axis=1)
    part_b = part.astype(jnp.bfloat16)
    summed = part
    for by in range(1, n_ch):
        pairs = [(i, (i + by) % n_ch) for i in range(n_ch)]
        summed = summed + lax.ppermute(part_b, "ch", pairs).astype(jnp.float32)
    rank = step_down.shape[1]
    step_low = summed[:, :rank].astype(jnp.bfloat16)
    state_terms = summed[:, rank:]

    tiles = channels // TILE
    f32, bf16 = jnp.float32, jnp.bfloat16
    whole = lambda shape: pl.BlockSpec(shape, lambda i: (0,) * len(shape))
    cols = lambda r: pl.BlockSpec((r, TILE), lambda i: (0, i))
    tile_rows = rows * SUBS
    params = pltpu.CompilerParams(vmem_limit_bytes=32 * 1024 * 1024)
    step_rows, end_state, totals = pl.pallas_call(
        first_pass,
        grid=(tiles,),
        in_specs=[whole((rows, rank)), cols(rank), cols(1), cols(rows), whole((rows, 2 * STATE)),
                  cols(STATE)],
        out_specs=[
            pl.BlockSpec((1, tile_rows, LANES), lambda i: (i, 0, 0)),
            pl.BlockSpec((1, STATE, SUBS, LANES), lambda i: (i, 0, 0, 0)),
            pl.BlockSpec((1, SUBS, LANES), lambda i: (i, 0, 0)),
        ],
        out_shape=[
            jax.ShapeDtypeStruct((tiles, tile_rows, LANES), f32),
            jax.ShapeDtypeStruct((tiles, STATE, SUBS, LANES), f32),
            jax.ShapeDtypeStruct((tiles, SUBS, LANES), f32),
        ],
        scratch_shapes=[
            pltpu.VMEM((STATE * rows, LANES), f32),
            pltpu.VMEM((tile_rows, LANES), f32),
            pltpu.VMEM((STATE * SUBS, LANES), f32),
        ],
        compiler_params=params,
        name="first_pass",
    )(step_low, step_up, step_bias[None], activation, state_terms, decay_rate)

    splits = max(1, n_ctx * LANES // channels)
    groups, held = n_ctx // splits, STATE // splits
    chunk = channels // groups
    subs = chunk // LANES
    per_tile = SUBS // subs
    rows_state = held * subs
    rows_back = -(-rows_state // 16) * 16
    rows_all = -(-(rows_state + 2 * subs) // 16) * 16
    ends = end_state.reshape(tiles, splits, held, per_tile, subs, LANES).transpose(0, 3, 1, 2, 4, 5)
    ends = ends.reshape(n_ctx, rows_state, LANES).astype(bf16)
    total = jnp.repeat(totals.reshape(groups, subs, LANES), splits, axis=0)
    total_hi = total.astype(bf16)
    total_lo = (total - total_hi.astype(f32)).astype(bf16)
    fill = jnp.zeros((n_ctx, rows_all - rows_state - 2 * subs, LANES), bf16)
    packed = jnp.concatenate([ends, total_hi, total_lo, fill], axis=1)
    me = lax.axis_index("ctx")
    my_rate = lax.dynamic_slice(
        decay_rate, (me % splits * held, me // splits * chunk), (held, chunk))
    my_rate = (my_rate * (-LOG2E)).reshape(rows_state, LANES)
    incoming = pl.pallas_call(
        functools.partial(exchange, n_ctx, rows_state, subs),
        in_specs=[pl.BlockSpec(memory_space=pltpu.VMEM)] * 2,
        out_specs=pl.BlockSpec(memory_space=pltpu.VMEM),
        out_shape=jax.ShapeDtypeStruct((n_ctx, rows_back, LANES), bf16),
        scratch_shapes=[
            pltpu.VMEM((n_ctx, rows_all, LANES), bf16),
            pltpu.VMEM((n_ctx, rows_back, LANES), bf16),
        ] + [pltpu.SemaphoreType.DMA((n_ctx,))] * 4,
        compiler_params=pltpu.CompilerParams(
            collective_id=0, has_side_effects=True, vmem_limit_bytes=32 * 1024 * 1024),
        name="exchange",
    )(packed, my_rate)
    incoming = incoming[:, :rows_state].reshape(tiles, per_tile, splits, held, subs, LANES)
    incoming = incoming.transpose(0, 2, 3, 1, 4, 5)
    incoming = incoming.reshape(tiles, STATE, SUBS, LANES).astype(f32)

    outgoing = pl.pallas_call(
        second_pass,
        grid=(tiles,),
        in_specs=[
            pl.BlockSpec((1, tile_rows, LANES), lambda i: (i, 0, 0)),
            cols(rows), whole((rows, 2 * STATE)), cols(STATE),
            pl.BlockSpec((1, STATE, SUBS, LANES), lambda i: (i, 0, 0, 0)),
            cols(rows), cols(1),
        ],
        out_specs=cols(rows),
        out_shape=jax.ShapeDtypeStruct((rows, channels), bf16),
        scratch_shapes=[
            pltpu.VMEM((2 * STATE * rows, LANES), f32),
            pltpu.VMEM((tile_rows, LANES), f32),
            pltpu.VMEM((STATE * SUBS, LANES), f32),
            pltpu.VMEM((tile_rows, LANES), f32),
        ],
        compiler_params=params,
        name="second_pass",
    )(step_rows, activation, state_terms, decay_rate, incoming, inner_gate, skip_gain[None])
    mamba_out = lax.all_to_all(outgoing, "ch", split_axis=0, concat_axis=1, tiled=True)
    attention_out = attend(queries, key_rows, value_rows)
    return (mamba_out, attention_out)


def solution(mesh):
    placed = (
        P(("ctx", "ch"), None),
        P(("ctx", "ch"), None),
        P(None, "ch"),
        P("ch"),
        P("ch", None),
        P("ch", None),
        P(None, "ch"),
        P("ch"),
        P(None, "ch"),
        P("ch"),
        P("ctx", "ch"),
        P("ctx", "ch"),
        P("ctx", "ch"),
    )
    return jax.shard_map(
        local,
        mesh=mesh,
        in_specs=placed,
        out_specs=(P(("ctx", "ch"), None), P("ctx", "ch")),
        check_vma=False,
    )
```

```python
import functools
import math

import jax
import jax.numpy as jnp
from jax import lax
from jax.experimental import pallas as pl
from jax.experimental.pallas import tpu as pltpu
from jax.sharding import PartitionSpec as P

STATE = 16
CONV = 4
HEADS = 64
KV_HEADS = 8
HEAD_DIM = 128


def halo(mamba_input, n_ctx, n_ch):
    width = mamba_input.shape[1] // n_ch
    tail = mamba_input[mamba_input.shape[0] - (CONV - 1) :]
    arrived = 0
    for j in range(n_ch):
        pairs = [(c * n_ch + n_ch - 1, (c + 1) * n_ch + j) for c in range(n_ctx - 1)]
        part = lax.ppermute(tail[:, j * width : (j + 1) * width], ("ctx", "ch"), pairs)
        arrived = arrived + part
    return arrived


LANES = 128
SUBS = 8
TILE = LANES * SUBS
LOG2E = math.log2(math.e)
MESH = pl.DeviceIdType.MESH


def to_rows(dst_ref, value):
    rows = value.shape[0]
    for sub in range(SUBS):
        dst_ref[pl.ds(sub, rows, stride=SUBS), :] = value[:, sub * LANES : (sub + 1) * LANES]


def spread_terms(terms_ref, spread_ref, count):
    rows = terms_ref.shape[0]
    for n in range(count):
        spread_ref[n * rows : (n + 1) * rows, :] = jnp.broadcast_to(
            terms_ref[:, n : n + 1], (rows, LANES)
        )


def row_of(spread_ref, index):
    return spread_ref[pl.ds(index, SUBS, stride=0), :]


def first_pass(packing, low_ref, up_ref, bias_ref, act_ref, terms_ref, decay_ref,
               step_ref, packed_ref, spread, act_rows, rates, pack):
    rows = act_ref.shape[0]

    @pl.when(pl.program_id(0) == 0)
    def _():
        spread_terms(terms_ref, spread, STATE)

    pre = jnp.dot(low_ref[...], up_ref[...], preferred_element_type=jnp.float32) + bias_ref[...]
    to_rows(step_ref.at[0], jax.nn.softplus(pre))
    to_rows(act_rows, act_ref[...].astype(jnp.float32))
    to_rows(rates, decay_ref[...] * (-LOG2E))
    rate = [rates[n * SUBS : (n + 1) * SUBS, :] for n in range(STATE)]

    def token(t, carry):
        states, total = carry
        at = pl.multiple_of(t * SUBS, SUBS)
        step = step_ref[0, pl.ds(at, SUBS), :]
        push = step * act_rows[pl.ds(at, SUBS), :]
        states = tuple(
            jnp.exp2(step * rate[n]) * states[n] + push * row_of(spread, n * rows + t)
            for n in range(STATE)
        )
        return states, total + step

    zero = jnp.zeros((SUBS, LANES), jnp.float32)
    states, total = lax.fori_loop(0, rows, token, ((zero,) * STATE, zero), unroll=4)
    splits, subs, held, rows_state = packing
    total_hi = total.astype(jnp.bfloat16).astype(jnp.float32)
    pack[...] = jnp.zeros_like(pack)
    for part in range(pack.shape[0]):
        cut = slice(part // splits * subs, (part // splits + 1) * subs)
        for n in range(held):
            pack[part, n * subs : (n + 1) * subs] = states[part % splits * held + n][cut]
        pack[part, rows_state : rows_state + subs] = total_hi[cut]
        pack[part, rows_state + subs : rows_state + 2 * subs] = (total - total_hi)[cut]
    packed_ref[...] = pack[...].astype(jnp.bfloat16)


def second_pass(packing, n_ch, step_ref, act_ref, terms_ref, decay_ref, incoming_ref, gate_ref, skip_ref,
                out_ref, spread, act_rows, rates, outs, entering, wide, outbox,
                keep_sem, send_sem, recv_sem):
    rows = act_ref.shape[0]
    splits, subs, held, rows_state = packing
    tile, tiles = pl.program_id(0), pl.num_programs(0)
    me = lax.axis_index("ch")
    here = outbox.shape[1]
    channels = outbox.shape[2]

    @pl.when(tile == 0)
    def _():
        barrier = pltpu.get_barrier_semaphore()
        for k in range(1, n_ch):
            peer = lax.rem(me + k, n_ch)
            pl.semaphore_signal(barrier, inc=1, device_id={"ch": peer}, device_id_type=MESH)
        pl.semaphore_wait(barrier, n_ch - 1)
        spread_terms(terms_ref, spread, 2 * STATE)

    to_rows(act_rows, act_ref[...].astype(jnp.float32))
    to_rows(rates, decay_ref[...] * (-LOG2E))
    rate = [rates[n * SUBS : (n + 1) * SUBS, :] for n in range(STATE)]

    def token(t, states):
        at = pl.multiple_of(t * SUBS, SUBS)
        step = step_ref[0, pl.ds(at, SUBS), :]
        push = step * act_rows[pl.ds(at, SUBS), :]
        new, parts = [], []
        for n in range(STATE):
            state = jnp.exp2(step * rate[n]) * states[n] + push * row_of(spread, n * rows + t)
            new.append(state)
            term = state * row_of(spread, (STATE + n) * rows + t)
            if n < 2:
                parts.append(term)
            else:
                parts[n % 2] = parts[n % 2] + term
        outs[pl.ds(at, SUBS), :] = parts[0] + parts[1]
        return tuple(new)

    wide[...] = incoming_ref[...].astype(jnp.float32)
    for part in range(wide.shape[0]):
        for n in range(held):
            row = (part % splits * held + n) * SUBS + part // splits * subs
            entering[row : row + subs, :] = wide[part, n * subs : (n + 1) * subs]
    start = tuple(entering[n * SUBS : (n + 1) * SUBS, :] for n in range(STATE))
    lax.fori_loop(0, rows, token, start, unroll=4)
    first = pl.multiple_of(tile * TILE, TILE)
    for sub in range(SUBS):
        cols = slice(sub * LANES, (sub + 1) * LANES)
        mixed = outs[pl.ds(sub, rows, stride=SUBS), :]
        mixed = mixed + skip_ref[:, cols] * act_ref[:, cols].astype(jnp.float32)
        mixed = mixed.astype(jnp.bfloat16).astype(jnp.float32)
        mixed = mixed * jax.nn.silu(gate_ref[:, cols].astype(jnp.float32))
        mixed = mixed.astype(jnp.bfloat16)
        at = pl.multiple_of(first + sub * LANES, LANES)
        for j in range(n_ch):
            outbox[j, :, pl.ds(at, LANES)] = mixed[j * here : (j + 1) * here]

    def keep(i):
        source = pl.multiple_of(i * TILE, TILE)
        target = pl.multiple_of(me * channels + i * TILE, TILE)
        return pltpu.make_async_copy(
            outbox.at[me, :, pl.ds(source, TILE)], out_ref.at[:, pl.ds(target, TILE)],
            keep_sem.at[i])

    def send(i, k):
        peer = lax.rem(me + k, n_ch)
        source = pl.multiple_of(i * TILE, TILE)
        target = pl.multiple_of(me * channels + i * TILE, TILE)
        return pltpu.make_async_remote_copy(
            src_ref=outbox.at[peer, :, pl.ds(source, TILE)],
            dst_ref=out_ref.at[:, pl.ds(target, TILE)],
            send_sem=send_sem.at[i, k], recv_sem=recv_sem.at[i, k],
            device_id={"ch": peer}, device_id_type=MESH)

    for k in range(1, n_ch):
        send(tile, k).start()
    keep(tile).start()

    @pl.when(tile == tiles - 1)
    def _():
        @pl.loop(0, tiles)
        def _(i):
            for k in range(1, n_ch):
                send(i, k).wait()
            keep(i).wait()


def exchange(n_ctx, rows_state, rows_total, send_ref, rate_ref, q_ref, k_ref, v_ref,
             back_ref, mixed_ref, got, reply, send_sem, got_sem, reply_sem, back_sem):
    me = lax.axis_index("ctx")
    rows = q_ref.shape[0]
    groups = k_ref.shape[1] // HEAD_DIM
    block = q_ref.shape[1] // groups

    def attend(g, carry):
        at = pl.ds(pl.multiple_of(g * HEAD_DIM, HEAD_DIM), HEAD_DIM)
        first = pl.multiple_of(g * block, HEAD_DIM)
        parts = attend_group(
            me * rows, rows, q_ref[:, pl.ds(first, block)], k_ref[:, at], v_ref[:, at])
        for h, part in enumerate(parts):
            mixed_ref[:, pl.ds(pl.multiple_of(first + h * HEAD_DIM, HEAD_DIM), HEAD_DIM)] = part
        return carry

    barrier = pltpu.get_barrier_semaphore()
    for k in range(1, n_ctx):
        peer = lax.rem(me + k, n_ctx)
        pl.semaphore_signal(barrier, inc=1, device_id={"ctx": peer}, device_id_type=MESH)
    pl.semaphore_wait(barrier, n_ctx - 1)

    def there(k):
        peer = lax.rem(me + k, n_ctx)
        return pltpu.make_async_remote_copy(
            src_ref=send_ref.at[peer], dst_ref=got.at[me], send_sem=send_sem.at[k],
            recv_sem=got_sem.at[k], device_id={"ctx": peer}, device_id_type=MESH)

    def back(k):
        peer = lax.rem(me + k, n_ctx)
        return pltpu.make_async_remote_copy(
            src_ref=reply.at[peer], dst_ref=back_ref.at[me], send_sem=reply_sem.at[k],
            recv_sem=back_sem.at[k], device_id={"ctx": peer}, device_id_type=MESH)

    for k in range(1, n_ctx):
        there(k).start()
    got[me] = send_ref[me]
    half = (groups + 1) // 2
    lax.fori_loop(0, half, attend, 0)
    for k in range(1, n_ctx):
        there(k).wait()

    state_shape = (rows_state, LANES)
    reps = rows_state // rows_total

    def combine(i, carry):
        sent = carry
        if reply.shape[1] > rows_state:
            spare = jnp.zeros((reply.shape[1] - rows_state, LANES), jnp.float32)
            sent = jnp.concatenate([carry, spare], axis=0)
        reply[i] = sent.astype(jnp.bfloat16)
        block = got[i].astype(jnp.float32)
        total = (block[rows_state : rows_state + rows_total]
                 + block[rows_state + rows_total : rows_state + 2 * rows_total])
        wide = jnp.concatenate([total] * reps, axis=0)
        return jnp.exp2(rate_ref[...] * wide) * carry + block[:rows_state]

    lax.fori_loop(0, n_ctx, combine, jnp.zeros(state_shape, jnp.float32))
    for k in range(1, n_ctx):
        back(k).start()
    back_ref[me] = reply[me]
    lax.fori_loop(half, groups, attend, 0)
    for k in range(1, n_ctx):
        back(k).wait()


def attend_group(query_first, rows, q, k, v):
    heads = q.shape[1] // HEAD_DIM
    stacked = jnp.concatenate(
        [q[:, h * HEAD_DIM : (h + 1) * HEAD_DIM] for h in range(heads)], axis=0
    )
    scores = lax.dot_general(
        stacked, k, (((1,), (1,)), ((), ())), preferred_element_type=jnp.float32
    ) * (LOG2E / math.sqrt(HEAD_DIM))
    query_pos = query_first + lax.broadcasted_iota(jnp.int32, scores.shape, 0) % rows
    visible = lax.broadcasted_iota(jnp.int32, scores.shape, 1) <= query_pos
    masked = jnp.where(visible, scores, -1e30)
    weights = jnp.exp2(masked - jnp.max(masked, axis=1, keepdims=True))
    total = jnp.sum(weights, axis=1, keepdims=True)
    mixed = jnp.dot(weights.astype(jnp.bfloat16), v, preferred_element_type=jnp.float32) / total
    mixed = mixed.astype(jnp.bfloat16)
    return [mixed[h * rows : (h + 1) * rows] for h in range(heads)]


def local(
    mamba_input, mamba_gate, conv_weight, conv_bias, step_down, state_proj, step_up, step_bias,
    decay_rate, skip_gain, queries, key_rows, value_rows,
):
    n_ctx, n_ch = lax.axis_size("ctx"), lax.axis_size("ch")
    keys = lax.all_gather(key_rows, "ctx", axis=0, tiled=True)
    values = lax.all_gather(value_rows, "ctx", axis=0, tiled=True)
    inner_in = lax.all_to_all(mamba_input, "ch", split_axis=1, concat_axis=0, tiled=True)
    inner_gate = lax.all_to_all(mamba_gate, "ch", split_axis=1, concat_axis=0, tiled=True)
    rows, channels = inner_in.shape
    rim_rows = halo(mamba_input, n_ctx, n_ch)
    padded = jnp.concatenate([rim_rows, inner_in], axis=0).astype(jnp.float32)
    conv_sum = conv_bias[None, :] + sum(
        conv_weight[tap][None, :] * padded[tap : tap + rows] for tap in range(CONV)
    )
    activation = jax.nn.silu(conv_sum).astype(jnp.bfloat16)
    low_part = jnp.dot(activation, step_down, preferred_element_type=jnp.float32)
    term_part = jnp.dot(activation, state_proj, preferred_element_type=jnp.float32)
    part = jnp.concatenate([low_part, term_part], axis=1)
    part_b = part.astype(jnp.bfloat16)
    summed = part
    for by in range(1, n_ch):
        pairs = [(i, (i + by) % n_ch) for i in range(n_ch)]
        summed = summed + lax.ppermute(part_b, "ch", pairs).astype(jnp.float32)
    rank = step_down.shape[1]
    step_low = summed[:, :rank].astype(jnp.bfloat16)
    state_terms = summed[:, rank:]

    tiles = channels // TILE
    f32, bf16 = jnp.float32, jnp.bfloat16
    whole = lambda shape: pl.BlockSpec(shape, lambda i: (0,) * len(shape))
    cols = lambda r: pl.BlockSpec((r, TILE), lambda i: (0, i))
    step_spec = pl.BlockSpec((1, rows * SUBS, LANES), lambda i: (i, 0, 0))
    limit = 32 * 1024 * 1024
    tile_rows = rows * SUBS
    splits = max(1, n_ctx * LANES // channels)
    groups, held = n_ctx // splits, STATE // splits
    chunk = channels // groups
    subs = chunk // LANES
    parts = n_ctx // tiles
    rows_state = held * subs
    rows_back = -(-rows_state // 16) * 16
    rows_all = -(-(rows_state + 2 * subs) // 16) * 16
    packing = (splits, subs, held, rows_state)
    step_rows, packed = pl.pallas_call(
        functools.partial(first_pass, packing),
        grid=(tiles,),
        in_specs=[whole((rows, rank)), cols(rank), cols(1), cols(rows), whole((rows, 2 * STATE)),
                  cols(STATE)],
        out_specs=[step_spec, pl.BlockSpec((parts, rows_all, LANES), lambda i: (i, 0, 0))],
        out_shape=[
            jax.ShapeDtypeStruct((tiles, tile_rows, LANES), f32),
            jax.ShapeDtypeStruct((n_ctx, rows_all, LANES), bf16),
        ],
        scratch_shapes=[
            pltpu.VMEM((STATE * rows, LANES), f32),
            pltpu.VMEM((tile_rows, LANES), f32),
            pltpu.VMEM((STATE * SUBS, LANES), f32),
            pltpu.VMEM((parts, rows_all, LANES), f32),
        ],
        compiler_params=pltpu.CompilerParams(vmem_limit_bytes=limit),
        name="first_pass",
    )(step_low, step_up, step_bias[None], activation, state_terms, decay_rate)

    me = lax.axis_index("ctx")
    my_rate = lax.dynamic_slice(
        decay_rate, (me % splits * held, me // splits * chunk), (held, chunk))
    my_rate = (my_rate * (-LOG2E)).reshape(rows_state, LANES)
    vmem = pl.BlockSpec(memory_space=pltpu.VMEM)
    incoming, attention_out = pl.pallas_call(
        functools.partial(exchange, n_ctx, rows_state, subs),
        in_specs=[vmem] * 5,
        out_specs=[vmem] * 2,
        out_shape=[
            jax.ShapeDtypeStruct((n_ctx, rows_back, LANES), bf16),
            jax.ShapeDtypeStruct(queries.shape, bf16),
        ],
        scratch_shapes=[
            pltpu.VMEM((n_ctx, rows_all, LANES), bf16),
            pltpu.VMEM((n_ctx, rows_back, LANES), bf16),
        ] + [pltpu.SemaphoreType.DMA((n_ctx,))] * 4,
        compiler_params=pltpu.CompilerParams(
            collective_id=0, has_side_effects=True, vmem_limit_bytes=limit),
        name="exchange",
    )(packed, my_rate, queries, keys, values)

    mamba_out = pl.pallas_call(
        functools.partial(second_pass, packing, n_ch),
        grid=(tiles,),
        in_specs=[
            step_spec, cols(rows), whole((rows, 2 * STATE)), cols(STATE),
            pl.BlockSpec((parts, rows_back, LANES), lambda i: (i, 0, 0)),
            cols(rows), cols(1),
        ],
        out_specs=pl.BlockSpec(memory_space=pl.ANY),
        out_shape=jax.ShapeDtypeStruct(mamba_input.shape, bf16),
        scratch_shapes=[
            pltpu.VMEM((2 * STATE * rows, LANES), f32),
            pltpu.VMEM((tile_rows, LANES), f32),
            pltpu.VMEM((STATE * SUBS, LANES), f32),
            pltpu.VMEM((tile_rows, LANES), f32),
            pltpu.VMEM((STATE * SUBS, LANES), f32),
            pltpu.VMEM((parts, rows_back, LANES), f32),
            pltpu.VMEM((n_ch, rows // n_ch, channels), bf16),
            pltpu.SemaphoreType.DMA((tiles,)),
            pltpu.SemaphoreType.DMA((tiles, n_ch)),
            pltpu.SemaphoreType.DMA((tiles, n_ch)),
        ],
        compiler_params=pltpu.CompilerParams(
            collective_id=1, has_side_effects=True, vmem_limit_bytes=limit),
        name="second_pass",
    )(step_rows, activation, state_terms, decay_rate, incoming, inner_gate, skip_gain[None])
    return (mamba_out, attention_out)


def solution(mesh):
    placed = (
        P(("ctx", "ch"), None),
        P(("ctx", "ch"), None),
        P(None, "ch"),
        P("ch"),
        P("ch", None),
        P("ch", None),
        P(None, "ch"),
        P("ch"),
        P(None, "ch"),
        P("ch"),
        P("ctx", "ch"),
        P("ctx", "ch"),
        P("ctx", "ch"),
    )
    return jax.shard_map(
        local,
        mesh=mesh,
        in_specs=placed,
        out_specs=(P(("ctx", "ch"), None), P("ctx", "ch")),
        check_vma=False,
    )
```

```python
import functools
import math

import jax
import jax.numpy as jnp
from jax import lax
from jax.experimental import pallas as pl
from jax.experimental.pallas import tpu as pltpu
from jax.sharding import PartitionSpec as P

STATE = 16
CONV = 4
HEADS = 64
KV_HEADS = 8
HEAD_DIM = 128


def halo(mamba_input, n_ctx, n_ch):
    width = mamba_input.shape[1] // n_ch
    tail = mamba_input[mamba_input.shape[0] - (CONV - 1) :]
    arrived = 0
    for j in range(n_ch):
        pairs = [(c * n_ch + n_ch - 1, (c + 1) * n_ch + j) for c in range(n_ctx - 1)]
        part = lax.ppermute(tail[:, j * width : (j + 1) * width], ("ctx", "ch"), pairs)
        arrived = arrived + part
    return arrived


LANES = 128
SUBS = 8
TILE = LANES * SUBS
LOG2E = math.log2(math.e)
MESH = pl.DeviceIdType.MESH


def to_rows(dst_ref, value):
    rows = value.shape[0]
    for sub in range(SUBS):
        dst_ref[pl.ds(sub, rows, stride=SUBS), :] = value[:, sub * LANES : (sub + 1) * LANES]


def spread_terms(terms_ref, spread_ref, count):
    rows = terms_ref.shape[0]
    for n in range(count):
        spread_ref[n * rows : (n + 1) * rows, :] = jnp.broadcast_to(
            terms_ref[:, n : n + 1], (rows, LANES)
        )


def row_of(spread_ref, index):
    return spread_ref[pl.ds(index, SUBS, stride=0), :]


def first_pass(packing, low_ref, up_ref, bias_ref, act_ref, terms_ref, decay_ref,
               step_ref, packed_ref, spread, act_rows, rates, pack):
    rows = act_ref.shape[0]

    @pl.when(pl.program_id(0) == 0)
    def _():
        spread_terms(terms_ref, spread, STATE)

    pre = jnp.dot(low_ref[...], up_ref[...], preferred_element_type=jnp.float32) + bias_ref[...]
    to_rows(step_ref.at[0], jax.nn.softplus(pre))
    to_rows(act_rows, act_ref[...].astype(jnp.float32))
    to_rows(rates, decay_ref[...] * (-LOG2E))
    rate = [rates[n * SUBS : (n + 1) * SUBS, :] for n in range(STATE)]

    def token(t, carry):
        states, total = carry
        at = pl.multiple_of(t * SUBS, SUBS)
        step = step_ref[0, pl.ds(at, SUBS), :]
        push = step * act_rows[pl.ds(at, SUBS), :]
        states = tuple(
            jnp.exp2(step * rate[n]) * states[n] + push * row_of(spread, n * rows + t)
            for n in range(STATE)
        )
        return states, total + step

    zero = jnp.zeros((SUBS, LANES), jnp.float32)
    states, total = lax.fori_loop(0, rows, token, ((zero,) * STATE, zero), unroll=4)
    splits, subs, held, rows_state = packing
    total_hi = total.astype(jnp.bfloat16).astype(jnp.float32)
    pack[...] = jnp.zeros_like(pack)
    for part in range(pack.shape[0]):
        cut = slice(part // splits * subs, (part // splits + 1) * subs)
        for n in range(held):
            pack[part, n * subs : (n + 1) * subs] = states[part % splits * held + n][cut]
        pack[part, rows_state : rows_state + subs] = total_hi[cut]
        pack[part, rows_state + subs : rows_state + 2 * subs] = (total - total_hi)[cut]
    packed_ref[...] = pack[...].astype(jnp.bfloat16)


def second_pass(packing, n_ch, step_ref, act_ref, terms_ref, decay_ref, incoming_ref, gate_ref, skip_ref,
                out_ref, spread, act_rows, rates, outs, entering, wide, outbox,
                keep_sem, send_sem, recv_sem):
    rows = act_ref.shape[0]
    splits, subs, held, rows_state = packing
    tile, tiles = pl.program_id(0), pl.num_programs(0)
    me = lax.axis_index("ch")
    here = outbox.shape[1]
    channels = outbox.shape[2]

    @pl.when(tile == 0)
    def _():
        barrier = pltpu.get_barrier_semaphore()
        for k in range(1, n_ch):
            peer = lax.rem(me + k, n_ch)
            pl.semaphore_signal(barrier, inc=1, device_id={"ch": peer}, device_id_type=MESH)
        pl.semaphore_wait(barrier, n_ch - 1)
        spread_terms(terms_ref, spread, 2 * STATE)

    to_rows(act_rows, act_ref[...].astype(jnp.float32))
    to_rows(rates, decay_ref[...] * (-LOG2E))
    rate = [rates[n * SUBS : (n + 1) * SUBS, :] for n in range(STATE)]

    def token(t, states):
        at = pl.multiple_of(t * SUBS, SUBS)
        step = step_ref[0, pl.ds(at, SUBS), :]
        push = step * act_rows[pl.ds(at, SUBS), :]
        new, parts = [], []
        for n in range(STATE):
            state = jnp.exp2(step * rate[n]) * states[n] + push * row_of(spread, n * rows + t)
            new.append(state)
            term = state * row_of(spread, (STATE + n) * rows + t)
            if n < 2:
                parts.append(term)
            else:
                parts[n % 2] = parts[n % 2] + term
        outs[pl.ds(at, SUBS), :] = parts[0] + parts[1]
        return tuple(new)

    wide[...] = incoming_ref[...].astype(jnp.float32)
    for part in range(wide.shape[0]):
        for n in range(held):
            row = (part % splits * held + n) * SUBS + part // splits * subs
            entering[row : row + subs, :] = wide[part, n * subs : (n + 1) * subs]
    start = tuple(entering[n * SUBS : (n + 1) * SUBS, :] for n in range(STATE))
    lax.fori_loop(0, rows, token, start, unroll=4)
    first = pl.multiple_of(tile * TILE, TILE)
    for sub in range(SUBS):
        cols = slice(sub * LANES, (sub + 1) * LANES)
        mixed = outs[pl.ds(sub, rows, stride=SUBS), :]
        mixed = mixed + skip_ref[:, cols] * act_ref[:, cols].astype(jnp.float32)
        mixed = mixed.astype(jnp.bfloat16).astype(jnp.float32)
        mixed = mixed * jax.nn.silu(gate_ref[:, cols].astype(jnp.float32))
        mixed = mixed.astype(jnp.bfloat16)
        at = pl.multiple_of(first + sub * LANES, LANES)
        for j in range(n_ch):
            outbox[j, :, pl.ds(at, LANES)] = mixed[j * here : (j + 1) * here]

    def keep(i):
        source = pl.multiple_of(i * TILE, TILE)
        target = pl.multiple_of(me * channels + i * TILE, TILE)
        return pltpu.make_async_copy(
            outbox.at[me, :, pl.ds(source, TILE)], out_ref.at[:, pl.ds(target, TILE)],
            keep_sem.at[i])

    def send(i, k):
        peer = lax.rem(me + k, n_ch)
        source = pl.multiple_of(i * TILE, TILE)
        target = pl.multiple_of(me * channels + i * TILE, TILE)
        return pltpu.make_async_remote_copy(
            src_ref=outbox.at[peer, :, pl.ds(source, TILE)],
            dst_ref=out_ref.at[:, pl.ds(target, TILE)],
            send_sem=send_sem.at[i, k], recv_sem=recv_sem.at[i, k],
            device_id={"ch": peer}, device_id_type=MESH)

    for k in range(1, n_ch):
        send(tile, k).start()
    keep(tile).start()

    @pl.when(tile == tiles - 1)
    def _():
        @pl.loop(0, tiles)
        def _(i):
            for k in range(1, n_ch):
                send(i, k).wait()
            keep(i).wait()


def swap_copies(n_ch, src_ref, dst_ref, keep_sem, send_sem, recv_sem):
    me = lax.axis_index("ch")
    width = dst_ref.shape[2]
    mine = pl.ds(pl.multiple_of(me * width, width), width)
    copies = []
    for k in range(1, n_ch):
        peer = lax.rem(me + k, n_ch)
        theirs = pl.ds(pl.multiple_of(peer * width, width), width)
        copies.append(pltpu.make_async_remote_copy(
            src_ref=src_ref.at[:, theirs], dst_ref=dst_ref.at[me], send_sem=send_sem.at[k],
            recv_sem=recv_sem.at[k], device_id={"ch": peer}, device_id_type=MESH))
    copies.append(pltpu.make_async_copy(src_ref.at[:, mine], dst_ref.at[me], keep_sem))
    return copies


def greet(axis, size):
    me = lax.axis_index(axis)
    for k in range(1, size):
        peer = lax.rem(me + k, size)
        pl.semaphore_signal(
            pltpu.get_barrier_semaphore(), inc=1, device_id={axis: peer}, device_id_type=MESH)


def swap_input(n_ch, src_ref, dst_ref, keep_sem, send_sem, recv_sem):
    greet("ch", n_ch)
    pl.semaphore_wait(pltpu.get_barrier_semaphore(), n_ch - 1)
    copies = swap_copies(n_ch, src_ref, dst_ref, keep_sem, send_sem, recv_sem)
    for copy in copies:
        copy.start()
    for copy in copies:
        copy.wait()


def exchange(n_ctx, n_ch, rows_state, rows_total, send_ref, rate_ref, q_ref, kv_ref, gate_ref,
             back_ref, mixed_ref, gate_out, got, reply, send_sem, got_sem, reply_sem, back_sem,
             keep_sem, gate_send, gate_recv):
    me = lax.axis_index("ctx")
    rows = q_ref.shape[0]
    groups = kv_ref.shape[1] // 2 // HEAD_DIM
    block = q_ref.shape[1] // groups

    def attend(g, carry):
        k_at = pl.ds(pl.multiple_of(g * HEAD_DIM, HEAD_DIM), HEAD_DIM)
        v_at = pl.ds(pl.multiple_of((groups + g) * HEAD_DIM, HEAD_DIM), HEAD_DIM)
        first = pl.multiple_of(g * block, HEAD_DIM)
        parts = attend_group(
            me * rows, rows, q_ref[:, pl.ds(first, block)], kv_ref[:, k_at], kv_ref[:, v_at])
        for h, part in enumerate(parts):
            mixed_ref[:, pl.ds(pl.multiple_of(first + h * HEAD_DIM, HEAD_DIM), HEAD_DIM)] = part
        return carry

    greet("ctx", n_ctx)
    greet("ch", n_ch)
    pl.semaphore_wait(pltpu.get_barrier_semaphore(), n_ctx + n_ch - 2)
    gates = swap_copies(n_ch, gate_ref, gate_out, keep_sem, gate_send, gate_recv)

    def there(k):
        peer = lax.rem(me + k, n_ctx)
        return pltpu.make_async_remote_copy(
            src_ref=send_ref.at[peer], dst_ref=got.at[me], send_sem=send_sem.at[k],
            recv_sem=got_sem.at[k], device_id={"ctx": peer}, device_id_type=MESH)

    def back(k):
        peer = lax.rem(me + k, n_ctx)
        return pltpu.make_async_remote_copy(
            src_ref=reply.at[peer], dst_ref=back_ref.at[me], send_sem=reply_sem.at[k],
            recv_sem=back_sem.at[k], device_id={"ctx": peer}, device_id_type=MESH)

    for k in range(1, n_ctx):
        there(k).start()
    for copy in gates:
        copy.start()
    got[me] = send_ref[me]
    half = (groups + 1) // 2
    lax.fori_loop(0, half, attend, 0)
    for k in range(1, n_ctx):
        there(k).wait()

    state_shape = (rows_state, LANES)
    reps = rows_state // rows_total

    def combine(i, carry):
        sent = carry
        if reply.shape[1] > rows_state:
            spare = jnp.zeros((reply.shape[1] - rows_state, LANES), jnp.float32)
            sent = jnp.concatenate([carry, spare], axis=0)
        reply[i] = sent.astype(jnp.bfloat16)
        block = got[i].astype(jnp.float32)
        total = (block[rows_state : rows_state + rows_total]
                 + block[rows_state + rows_total : rows_state + 2 * rows_total])
        wide = jnp.concatenate([total] * reps, axis=0)
        return jnp.exp2(rate_ref[...] * wide) * carry + block[:rows_state]

    lax.fori_loop(0, n_ctx, combine, jnp.zeros(state_shape, jnp.float32))
    for k in range(1, n_ctx):
        back(k).start()
    back_ref[me] = reply[me]
    lax.fori_loop(half, groups, attend, 0)
    for k in range(1, n_ctx):
        back(k).wait()
    for copy in gates:
        copy.wait()


def attend_group(query_first, rows, q, k, v):
    heads = q.shape[1] // HEAD_DIM
    stacked = jnp.concatenate(
        [q[:, h * HEAD_DIM : (h + 1) * HEAD_DIM] for h in range(heads)], axis=0
    )
    scores = lax.dot_general(
        stacked, k, (((1,), (1,)), ((), ())), preferred_element_type=jnp.float32
    ) * (LOG2E / math.sqrt(HEAD_DIM))
    query_pos = query_first + lax.broadcasted_iota(jnp.int32, scores.shape, 0) % rows
    visible = lax.broadcasted_iota(jnp.int32, scores.shape, 1) <= query_pos
    masked = jnp.where(visible, scores, -1e30)
    weights = jnp.exp2(masked - jnp.max(masked, axis=1, keepdims=True))
    total = jnp.sum(weights, axis=1, keepdims=True)
    mixed = jnp.dot(weights.astype(jnp.bfloat16), v, preferred_element_type=jnp.float32) / total
    mixed = mixed.astype(jnp.bfloat16)
    return [mixed[h * rows : (h + 1) * rows] for h in range(heads)]


def local(
    mamba_input, mamba_gate, conv_weight, conv_bias, step_down, state_proj, step_up, step_bias,
    decay_rate, skip_gain, queries, key_rows, value_rows,
):
    n_ctx, n_ch = lax.axis_size("ctx"), lax.axis_size("ch")
    kv = lax.all_gather(
        jnp.concatenate([key_rows, value_rows], axis=1), "ctx", axis=0, tiled=True)
    here, channels = mamba_input.shape[0], mamba_input.shape[1] // n_ch
    rows = here * n_ch
    limit = 56 * 1024 * 1024
    hbm = pl.BlockSpec(memory_space=pl.ANY)
    swapped = jax.ShapeDtypeStruct((n_ch, here, channels), jnp.bfloat16)
    swap_sems = [pltpu.SemaphoreType.DMA, pltpu.SemaphoreType.DMA((n_ch,)),
                 pltpu.SemaphoreType.DMA((n_ch,))]
    inner_in = pl.pallas_call(
        functools.partial(swap_input, n_ch),
        in_specs=[hbm],
        out_specs=hbm,
        out_shape=swapped,
        scratch_shapes=swap_sems,
        compiler_params=pltpu.CompilerParams(collective_id=2, has_side_effects=True),
        name="swap_input",
    )(mamba_input).reshape(rows, channels)
    rim_rows = halo(mamba_input, n_ctx, n_ch)
    padded = jnp.concatenate([rim_rows, inner_in], axis=0).astype(jnp.float32)
    conv_sum = conv_bias[None, :] + sum(
        conv_weight[tap][None, :] * padded[tap : tap + rows] for tap in range(CONV)
    )
    activation = jax.nn.silu(conv_sum).astype(jnp.bfloat16)
    low_part = jnp.dot(activation, step_down, preferred_element_type=jnp.float32)
    term_part = jnp.dot(activation, state_proj, preferred_element_type=jnp.float32)
    part = jnp.concatenate([low_part, term_part], axis=1)
    part_b = part.astype(jnp.bfloat16)
    summed = part
    for by in range(1, n_ch):
        pairs = [(i, (i + by) % n_ch) for i in range(n_ch)]
        summed = summed + lax.ppermute(part_b, "ch", pairs).astype(jnp.float32)
    rank = step_down.shape[1]
    step_low = summed[:, :rank].astype(jnp.bfloat16)
    state_terms = summed[:, rank:]

    tiles = channels // TILE
    f32, bf16 = jnp.float32, jnp.bfloat16
    whole = lambda shape: pl.BlockSpec(shape, lambda i: (0,) * len(shape))
    cols = lambda r: pl.BlockSpec((r, TILE), lambda i: (0, i))
    step_spec = pl.BlockSpec((1, rows * SUBS, LANES), lambda i: (i, 0, 0))
    tile_rows = rows * SUBS
    splits = max(1, n_ctx * LANES // channels)
    groups, held = n_ctx // splits, STATE // splits
    chunk = channels // groups
    subs = chunk // LANES
    parts = n_ctx // tiles
    rows_state = held * subs
    rows_back = -(-rows_state // 16) * 16
    rows_all = -(-(rows_state + 2 * subs) // 16) * 16
    packing = (splits, subs, held, rows_state)
    step_rows, packed = pl.pallas_call(
        functools.partial(first_pass, packing),
        grid=(tiles,),
        in_specs=[whole((rows, rank)), cols(rank), cols(1), cols(rows), whole((rows, 2 * STATE)),
                  cols(STATE)],
        out_specs=[step_spec, pl.BlockSpec((parts, rows_all, LANES), lambda i: (i, 0, 0))],
        out_shape=[
            jax.ShapeDtypeStruct((tiles, tile_rows, LANES), f32),
            jax.ShapeDtypeStruct((n_ctx, rows_all, LANES), bf16),
        ],
        scratch_shapes=[
            pltpu.VMEM((STATE * rows, LANES), f32),
            pltpu.VMEM((tile_rows, LANES), f32),
            pltpu.VMEM((STATE * SUBS, LANES), f32),
            pltpu.VMEM((parts, rows_all, LANES), f32),
        ],
        compiler_params=pltpu.CompilerParams(vmem_limit_bytes=limit),
        name="first_pass",
    )(step_low, step_up, step_bias[None], activation, state_terms, decay_rate)

    me = lax.axis_index("ctx")
    my_rate = lax.dynamic_slice(
        decay_rate, (me % splits * held, me // splits * chunk), (held, chunk))
    my_rate = (my_rate * (-LOG2E)).reshape(rows_state, LANES)
    vmem = pl.BlockSpec(memory_space=pltpu.VMEM)
    incoming, attention_out, inner_gate = pl.pallas_call(
        functools.partial(exchange, n_ctx, n_ch, rows_state, subs),
        in_specs=[vmem] * 4 + [hbm],
        out_specs=[vmem] * 2 + [hbm],
        out_shape=[
            jax.ShapeDtypeStruct((n_ctx, rows_back, LANES), bf16),
            jax.ShapeDtypeStruct(queries.shape, bf16),
            swapped,
        ],
        scratch_shapes=[
            pltpu.VMEM((n_ctx, rows_all, LANES), bf16),
            pltpu.VMEM((n_ctx, rows_back, LANES), bf16),
        ] + [pltpu.SemaphoreType.DMA((n_ctx,))] * 4 + swap_sems,
        compiler_params=pltpu.CompilerParams(
            collective_id=0, has_side_effects=True, vmem_limit_bytes=limit),
        name="exchange",
    )(packed, my_rate, queries, kv, mamba_gate)

    mamba_out = pl.pallas_call(
        functools.partial(second_pass, packing, n_ch),
        grid=(tiles,),
        in_specs=[
            step_spec, cols(rows), whole((rows, 2 * STATE)), cols(STATE),
            pl.BlockSpec((parts, rows_back, LANES), lambda i: (i, 0, 0)),
            cols(rows), cols(1),
        ],
        out_specs=pl.BlockSpec(memory_space=pl.ANY),
        out_shape=jax.ShapeDtypeStruct(mamba_input.shape, bf16),
        scratch_shapes=[
            pltpu.VMEM((2 * STATE * rows, LANES), f32),
            pltpu.VMEM((tile_rows, LANES), f32),
            pltpu.VMEM((STATE * SUBS, LANES), f32),
            pltpu.VMEM((tile_rows, LANES), f32),
            pltpu.VMEM((STATE * SUBS, LANES), f32),
            pltpu.VMEM((parts, rows_back, LANES), f32),
            pltpu.VMEM((n_ch, rows // n_ch, channels), bf16),
            pltpu.SemaphoreType.DMA((tiles,)),
            pltpu.SemaphoreType.DMA((tiles, n_ch)),
            pltpu.SemaphoreType.DMA((tiles, n_ch)),
        ],
        compiler_params=pltpu.CompilerParams(
            collective_id=1, has_side_effects=True, vmem_limit_bytes=limit),
        name="second_pass",
    )(step_rows, activation, state_terms, decay_rate, incoming,
      inner_gate.reshape(rows, channels), skip_gain[None])
    return (mamba_out, attention_out)


def solution(mesh):
    placed = (
        P(("ctx", "ch"), None),
        P(("ctx", "ch"), None),
        P(None, "ch"),
        P("ch"),
        P("ch", None),
        P("ch", None),
        P(None, "ch"),
        P("ch"),
        P(None, "ch"),
        P("ch"),
        P("ctx", "ch"),
        P("ctx", "ch"),
        P("ctx", "ch"),
    )
    return jax.shard_map(
        local,
        mesh=mesh,
        in_specs=placed,
        out_specs=(P(("ctx", "ch"), None), P("ctx", "ch")),
        check_vma=False,
    )
```

```python
import functools
import math

import jax
import jax.numpy as jnp
from jax import lax
from jax.experimental import pallas as pl
from jax.experimental.pallas import tpu as pltpu
from jax.sharding import PartitionSpec as P

STATE = 16
CONV = 4
HEADS = 64
KV_HEADS = 8
HEAD_DIM = 128


def halo(mamba_input, n_ctx, n_ch):
    width = mamba_input.shape[1] // n_ch
    tail = mamba_input[mamba_input.shape[0] - (CONV - 1) :]
    arrived = 0
    for j in range(n_ch):
        pairs = [(c * n_ch + n_ch - 1, (c + 1) * n_ch + j) for c in range(n_ctx - 1)]
        part = lax.ppermute(tail[:, j * width : (j + 1) * width], ("ctx", "ch"), pairs)
        arrived = arrived + part
    return arrived


LANES = 128
SUBS = 8
TILE = LANES * SUBS
LOG2E = math.log2(math.e)
MESH = pl.DeviceIdType.MESH


def to_rows(dst_ref, value):
    rows = value.shape[0]
    for sub in range(SUBS):
        dst_ref[pl.ds(sub, rows, stride=SUBS), :] = value[:, sub * LANES : (sub + 1) * LANES]


def spread_terms(terms_ref, spread_ref, count):
    rows = terms_ref.shape[0]
    for n in range(count):
        spread_ref[n * rows : (n + 1) * rows, :] = jnp.broadcast_to(
            terms_ref[:, n : n + 1], (rows, LANES)
        )


def row_of(spread_ref, index):
    return spread_ref[pl.ds(index, SUBS, stride=0), :]


PIECES = 4


def swap_copies(n_ch, src_ref, dst_ref, keep_sem, send_sem, recv_sem):
    me = lax.axis_index("ch")
    width = dst_ref.shape[2]
    piece = width // PIECES
    copies = []
    for p in range(PIECES):
        target = pl.ds(p * piece, piece)
        for k in range(1, n_ch):
            peer = lax.rem(me + k, n_ch)
            source = pl.ds(pl.multiple_of(peer * width + p * piece, LANES), piece)
            copies.append(pltpu.make_async_remote_copy(
                src_ref=src_ref.at[:, source], dst_ref=dst_ref.at[me, :, target],
                send_sem=send_sem.at[p, k], recv_sem=recv_sem.at[p, k],
                device_id={"ch": peer}, device_id_type=MESH))
    mine = pl.ds(pl.multiple_of(me * width, LANES), width)
    copies.append(pltpu.make_async_copy(src_ref.at[:, mine], dst_ref.at[me], keep_sem))
    return copies


def greet(axis, size):
    me = lax.axis_index(axis)
    for k in range(1, size):
        peer = lax.rem(me + k, size)
        pl.semaphore_signal(
            pltpu.get_barrier_semaphore(), inc=1, device_id={axis: peer}, device_id_type=MESH)


def first_pass(packing, n_ch, low_ref, up_ref, bias_ref, act_ref, terms_ref, decay_ref, gate_ref,
               step_ref, packed_ref, gate_out, spread, act_rows, rates, pack,
               keep_sem, send_sem, recv_sem):
    rows = act_ref.shape[0]
    gates = swap_copies(n_ch, gate_ref, gate_out, keep_sem, send_sem, recv_sem)

    @pl.when(pl.program_id(0) == 0)
    def _():
        greet("ch", n_ch)
        pl.semaphore_wait(pltpu.get_barrier_semaphore(), n_ch - 1)
        for copy in gates:
            copy.start()

    @pl.when(pl.program_id(0) == 0)
    def _():
        spread_terms(terms_ref, spread, STATE)

    pre = jnp.dot(low_ref[...], up_ref[...], preferred_element_type=jnp.float32) + bias_ref[...]
    to_rows(step_ref.at[0], jax.nn.softplus(pre))
    to_rows(act_rows, act_ref[...].astype(jnp.float32))
    to_rows(rates, decay_ref[...] * (-LOG2E))
    rate = [rates[n * SUBS : (n + 1) * SUBS, :] for n in range(STATE)]

    def token(t, carry):
        states, total = carry
        at = pl.multiple_of(t * SUBS, SUBS)
        step = step_ref[0, pl.ds(at, SUBS), :]
        push = step * act_rows[pl.ds(at, SUBS), :]
        states = tuple(
            jnp.exp2(step * rate[n]) * states[n] + push * row_of(spread, n * rows + t)
            for n in range(STATE)
        )
        return states, total + step

    zero = jnp.zeros((SUBS, LANES), jnp.float32)
    states, total = lax.fori_loop(0, rows, token, ((zero,) * STATE, zero), unroll=8)
    splits, subs, held, rows_state = packing
    total_hi = total.astype(jnp.bfloat16).astype(jnp.float32)
    pack[...] = jnp.zeros_like(pack)
    for part in range(pack.shape[0]):
        cut = slice(part // splits * subs, (part // splits + 1) * subs)
        for n in range(held):
            pack[part, n * subs : (n + 1) * subs] = states[part % splits * held + n][cut]
        pack[part, rows_state : rows_state + subs] = total_hi[cut]
        pack[part, rows_state + subs : rows_state + 2 * subs] = (total - total_hi)[cut]
    packed_ref[...] = pack[...].astype(jnp.bfloat16)

    @pl.when(pl.program_id(0) == pl.num_programs(0) - 1)
    def _():
        for copy in gates:
            copy.wait()


def second_pass(packing, n_ch, step_ref, act_ref, terms_ref, decay_ref, incoming_ref, gate_ref, skip_ref,
                out_ref, spread, act_rows, rates, outs, entering, wide, outbox,
                keep_sem, send_sem, recv_sem):
    rows = act_ref.shape[0]
    splits, subs, held, rows_state = packing
    tile, tiles = pl.program_id(0), pl.num_programs(0)
    me = lax.axis_index("ch")
    here = outbox.shape[1]
    channels = outbox.shape[2]

    @pl.when(tile == 0)
    def _():
        barrier = pltpu.get_barrier_semaphore()
        for k in range(1, n_ch):
            peer = lax.rem(me + k, n_ch)
            pl.semaphore_signal(barrier, inc=1, device_id={"ch": peer}, device_id_type=MESH)
        pl.semaphore_wait(barrier, n_ch - 1)
        spread_terms(terms_ref, spread, 2 * STATE)

    to_rows(act_rows, act_ref[...].astype(jnp.float32))
    to_rows(rates, decay_ref[...] * (-LOG2E))
    rate = [rates[n * SUBS : (n + 1) * SUBS, :] for n in range(STATE)]

    def token(t, states):
        at = pl.multiple_of(t * SUBS, SUBS)
        step = step_ref[0, pl.ds(at, SUBS), :]
        push = step * act_rows[pl.ds(at, SUBS), :]
        new, parts = [], []
        for n in range(STATE):
            state = jnp.exp2(step * rate[n]) * states[n] + push * row_of(spread, n * rows + t)
            new.append(state)
            term = state * row_of(spread, (STATE + n) * rows + t)
            if n < 2:
                parts.append(term)
            else:
                parts[n % 2] = parts[n % 2] + term
        outs[pl.ds(at, SUBS), :] = parts[0] + parts[1]
        return tuple(new)

    wide[...] = incoming_ref[...].astype(jnp.float32)
    for part in range(wide.shape[0]):
        for n in range(held):
            row = (part % splits * held + n) * SUBS + part // splits * subs
            entering[row : row + subs, :] = wide[part, n * subs : (n + 1) * subs]
    start = tuple(entering[n * SUBS : (n + 1) * SUBS, :] for n in range(STATE))
    lax.fori_loop(0, rows, token, start, unroll=8)
    first = pl.multiple_of(tile * TILE, TILE)
    for sub in range(SUBS):
        cols = slice(sub * LANES, (sub + 1) * LANES)
        mixed = outs[pl.ds(sub, rows, stride=SUBS), :]
        mixed = mixed + skip_ref[:, cols] * act_ref[:, cols].astype(jnp.float32)
        mixed = mixed.astype(jnp.bfloat16).astype(jnp.float32)
        mixed = mixed * jax.nn.silu(gate_ref[:, cols].astype(jnp.float32))
        mixed = mixed.astype(jnp.bfloat16)
        at = pl.multiple_of(first + sub * LANES, LANES)
        for j in range(n_ch):
            outbox[j, :, pl.ds(at, LANES)] = mixed[j * here : (j + 1) * here]

    def keep(i):
        source = pl.multiple_of(i * TILE, TILE)
        target = pl.multiple_of(me * channels + i * TILE, TILE)
        return pltpu.make_async_copy(
            outbox.at[me, :, pl.ds(source, TILE)], out_ref.at[:, pl.ds(target, TILE)],
            keep_sem.at[i])

    def send(i, k):
        peer = lax.rem(me + k, n_ch)
        source = pl.multiple_of(i * TILE, TILE)
        target = pl.multiple_of(me * channels + i * TILE, TILE)
        return pltpu.make_async_remote_copy(
            src_ref=outbox.at[peer, :, pl.ds(source, TILE)],
            dst_ref=out_ref.at[:, pl.ds(target, TILE)],
            send_sem=send_sem.at[i, k], recv_sem=recv_sem.at[i, k],
            device_id={"ch": peer}, device_id_type=MESH)

    for k in range(1, n_ch):
        send(tile, k).start()
    keep(tile).start()

    @pl.when(tile == tiles - 1)
    def _():
        @pl.loop(0, tiles)
        def _(i):
            for k in range(1, n_ch):
                send(i, k).wait()
            keep(i).wait()


def swap_input(n_ch, src_ref, dst_ref, keep_sem, send_sem, recv_sem):
    greet("ch", n_ch)
    pl.semaphore_wait(pltpu.get_barrier_semaphore(), n_ch - 1)
    copies = swap_copies(n_ch, src_ref, dst_ref, keep_sem, send_sem, recv_sem)
    for copy in copies:
        copy.start()
    for copy in copies:
        copy.wait()


def exchange(n_ctx, rows_state, rows_total, send_ref, rate_ref, q_ref, kv_ref,
             back_ref, mixed_ref, got, reply, send_sem, got_sem, reply_sem, back_sem):
    me = lax.axis_index("ctx")
    rows = q_ref.shape[0]
    groups = kv_ref.shape[1] // 2 // HEAD_DIM
    block = q_ref.shape[1] // groups

    def attend(g, carry):
        k_at = pl.ds(pl.multiple_of(g * HEAD_DIM, HEAD_DIM), HEAD_DIM)
        v_at = pl.ds(pl.multiple_of((groups + g) * HEAD_DIM, HEAD_DIM), HEAD_DIM)
        first = pl.multiple_of(g * block, HEAD_DIM)
        parts = attend_group(
            me * rows, rows, q_ref[:, pl.ds(first, block)], kv_ref[:, k_at], kv_ref[:, v_at])
        for h, part in enumerate(parts):
            mixed_ref[:, pl.ds(pl.multiple_of(first + h * HEAD_DIM, HEAD_DIM), HEAD_DIM)] = part
        return carry

    greet("ctx", n_ctx)
    pl.semaphore_wait(pltpu.get_barrier_semaphore(), n_ctx - 1)

    def there(k):
        peer = lax.rem(me + k, n_ctx)
        return pltpu.make_async_remote_copy(
            src_ref=send_ref.at[peer], dst_ref=got.at[me], send_sem=send_sem.at[k],
            recv_sem=got_sem.at[k], device_id={"ctx": peer}, device_id_type=MESH)

    def back(k):
        peer = lax.rem(me + k, n_ctx)
        return pltpu.make_async_remote_copy(
            src_ref=reply.at[peer], dst_ref=back_ref.at[me], send_sem=reply_sem.at[k],
            recv_sem=back_sem.at[k], device_id={"ctx": peer}, device_id_type=MESH)

    for k in range(1, n_ctx):
        there(k).start()
    got[me] = send_ref[me]
    half = (groups + 1) // 2
    lax.fori_loop(0, half, attend, 0)
    for k in range(1, n_ctx):
        there(k).wait()

    state_shape = (rows_state, LANES)
    reps = rows_state // rows_total

    def combine(i, carry):
        sent = carry
        if reply.shape[1] > rows_state:
            spare = jnp.zeros((reply.shape[1] - rows_state, LANES), jnp.float32)
            sent = jnp.concatenate([carry, spare], axis=0)
        reply[i] = sent.astype(jnp.bfloat16)
        block = got[i].astype(jnp.float32)
        total = (block[rows_state : rows_state + rows_total]
                 + block[rows_state + rows_total : rows_state + 2 * rows_total])
        wide = jnp.concatenate([total] * reps, axis=0)
        return jnp.exp2(rate_ref[...] * wide) * carry + block[:rows_state]

    lax.fori_loop(0, n_ctx, combine, jnp.zeros(state_shape, jnp.float32))
    for k in range(1, n_ctx):
        back(k).start()
    back_ref[me] = reply[me]
    lax.fori_loop(half, groups, attend, 0)
    for k in range(1, n_ctx):
        back(k).wait()


def attend_group(query_first, rows, q, k, v):
    heads = q.shape[1] // HEAD_DIM
    stacked = jnp.concatenate(
        [q[:, h * HEAD_DIM : (h + 1) * HEAD_DIM] for h in range(heads)], axis=0
    )
    scores = lax.dot_general(
        stacked, k, (((1,), (1,)), ((), ())), preferred_element_type=jnp.float32
    ) * (LOG2E / math.sqrt(HEAD_DIM))
    query_pos = query_first + lax.broadcasted_iota(jnp.int32, scores.shape, 0) % rows
    visible = lax.broadcasted_iota(jnp.int32, scores.shape, 1) <= query_pos
    masked = jnp.where(visible, scores, -1e30)
    weights = jnp.exp2(masked - jnp.max(masked, axis=1, keepdims=True))
    total = jnp.sum(weights, axis=1, keepdims=True)
    mixed = jnp.dot(weights.astype(jnp.bfloat16), v, preferred_element_type=jnp.float32) / total
    mixed = mixed.astype(jnp.bfloat16)
    return [mixed[h * rows : (h + 1) * rows] for h in range(heads)]


def local(
    mamba_input, mamba_gate, conv_weight, conv_bias, step_down, state_proj, step_up, step_bias,
    decay_rate, skip_gain, queries, key_rows, value_rows,
):
    n_ctx, n_ch = lax.axis_size("ctx"), lax.axis_size("ch")
    kv = lax.all_gather(
        jnp.concatenate([key_rows, value_rows], axis=1), "ctx", axis=0, tiled=True)
    here, channels = mamba_input.shape[0], mamba_input.shape[1] // n_ch
    rows = here * n_ch
    limit = 56 * 1024 * 1024
    hbm = pl.BlockSpec(memory_space=pl.ANY)
    swapped = jax.ShapeDtypeStruct((n_ch, here, channels), jnp.bfloat16)
    swap_sems = [pltpu.SemaphoreType.DMA, pltpu.SemaphoreType.DMA((PIECES, n_ch)),
                 pltpu.SemaphoreType.DMA((PIECES, n_ch))]
    inner_in = pl.pallas_call(
        functools.partial(swap_input, n_ch),
        in_specs=[hbm],
        out_specs=hbm,
        out_shape=swapped,
        scratch_shapes=swap_sems,
        compiler_params=pltpu.CompilerParams(collective_id=2, has_side_effects=True),
        name="swap_input",
    )(mamba_input).reshape(rows, channels)
    rim_rows = halo(mamba_input, n_ctx, n_ch)
    padded = jnp.concatenate([rim_rows, inner_in], axis=0).astype(jnp.float32)
    conv_sum = conv_bias[None, :] + sum(
        conv_weight[tap][None, :] * padded[tap : tap + rows] for tap in range(CONV)
    )
    activation = jax.nn.silu(conv_sum).astype(jnp.bfloat16)
    low_part = jnp.dot(activation, step_down, preferred_element_type=jnp.float32)
    term_part = jnp.dot(activation, state_proj, preferred_element_type=jnp.float32)
    part = jnp.concatenate([low_part, term_part], axis=1)
    part_b = part.astype(jnp.bfloat16)
    summed = part
    for by in range(1, n_ch):
        pairs = [(i, (i + by) % n_ch) for i in range(n_ch)]
        summed = summed + lax.ppermute(part_b, "ch", pairs).astype(jnp.float32)
    rank = step_down.shape[1]
    step_low = summed[:, :rank].astype(jnp.bfloat16)
    state_terms = summed[:, rank:]

    tiles = channels // TILE
    f32, bf16 = jnp.float32, jnp.bfloat16
    whole = lambda shape: pl.BlockSpec(shape, lambda i: (0,) * len(shape))
    cols = lambda r: pl.BlockSpec((r, TILE), lambda i: (0, i))
    step_spec = pl.BlockSpec((1, rows * SUBS, LANES), lambda i: (i, 0, 0))
    tile_rows = rows * SUBS
    splits = max(1, n_ctx * LANES // channels)
    groups, held = n_ctx // splits, STATE // splits
    chunk = channels // groups
    subs = chunk // LANES
    parts = n_ctx // tiles
    rows_state = held * subs
    rows_back = -(-rows_state // 16) * 16
    rows_all = -(-(rows_state + 2 * subs) // 16) * 16
    packing = (splits, subs, held, rows_state)
    step_rows, packed, inner_gate = pl.pallas_call(
        functools.partial(first_pass, packing, n_ch),
        grid=(tiles,),
        in_specs=[whole((rows, rank)), cols(rank), cols(1), cols(rows), whole((rows, 2 * STATE)),
                  cols(STATE), hbm],
        out_specs=[step_spec, pl.BlockSpec((parts, rows_all, LANES), lambda i: (i, 0, 0)), hbm],
        out_shape=[
            jax.ShapeDtypeStruct((tiles, tile_rows, LANES), f32),
            jax.ShapeDtypeStruct((n_ctx, rows_all, LANES), bf16),
            swapped,
        ],
        scratch_shapes=[
            pltpu.VMEM((STATE * rows, LANES), f32),
            pltpu.VMEM((tile_rows, LANES), f32),
            pltpu.VMEM((STATE * SUBS, LANES), f32),
            pltpu.VMEM((parts, rows_all, LANES), f32),
        ] + swap_sems,
        compiler_params=pltpu.CompilerParams(
            collective_id=3, has_side_effects=True, vmem_limit_bytes=limit),
        name="first_pass",
    )(step_low, step_up, step_bias[None], activation, state_terms, decay_rate, mamba_gate)

    me = lax.axis_index("ctx")
    my_rate = lax.dynamic_slice(
        decay_rate, (me % splits * held, me // splits * chunk), (held, chunk))
    my_rate = (my_rate * (-LOG2E)).reshape(rows_state, LANES)
    vmem = pl.BlockSpec(memory_space=pltpu.VMEM)
    incoming, attention_out = pl.pallas_call(
        functools.partial(exchange, n_ctx, rows_state, subs),
        in_specs=[vmem] * 4,
        out_specs=[vmem] * 2,
        out_shape=[
            jax.ShapeDtypeStruct((n_ctx, rows_back, LANES), bf16),
            jax.ShapeDtypeStruct(queries.shape, bf16),
        ],
        scratch_shapes=[
            pltpu.VMEM((n_ctx, rows_all, LANES), bf16),
            pltpu.VMEM((n_ctx, rows_back, LANES), bf16),
        ] + [pltpu.SemaphoreType.DMA((n_ctx,))] * 4,
        compiler_params=pltpu.CompilerParams(
            collective_id=0, has_side_effects=True, vmem_limit_bytes=limit),
        name="exchange",
    )(packed, my_rate, queries, kv)

    mamba_out = pl.pallas_call(
        functools.partial(second_pass, packing, n_ch),
        grid=(tiles,),
        in_specs=[
            step_spec, cols(rows), whole((rows, 2 * STATE)), cols(STATE),
            pl.BlockSpec((parts, rows_back, LANES), lambda i: (i, 0, 0)),
            cols(rows), cols(1),
        ],
        out_specs=pl.BlockSpec(memory_space=pl.ANY),
        out_shape=jax.ShapeDtypeStruct(mamba_input.shape, bf16),
        scratch_shapes=[
            pltpu.VMEM((2 * STATE * rows, LANES), f32),
            pltpu.VMEM((tile_rows, LANES), f32),
            pltpu.VMEM((STATE * SUBS, LANES), f32),
            pltpu.VMEM((tile_rows, LANES), f32),
            pltpu.VMEM((STATE * SUBS, LANES), f32),
            pltpu.VMEM((parts, rows_back, LANES), f32),
            pltpu.VMEM((n_ch, rows // n_ch, channels), bf16),
            pltpu.SemaphoreType.DMA((tiles,)),
            pltpu.SemaphoreType.DMA((tiles, n_ch)),
            pltpu.SemaphoreType.DMA((tiles, n_ch)),
        ],
        compiler_params=pltpu.CompilerParams(
            collective_id=1, has_side_effects=True, vmem_limit_bytes=limit),
        name="second_pass",
    )(step_rows, activation, state_terms, decay_rate, incoming,
      inner_gate.reshape(rows, channels), skip_gain[None])
    return (mamba_out, attention_out)


def solution(mesh):
    placed = (
        P(("ctx", "ch"), None),
        P(("ctx", "ch"), None),
        P(None, "ch"),
        P("ch"),
        P("ch", None),
        P("ch", None),
        P(None, "ch"),
        P("ch"),
        P(None, "ch"),
        P("ch"),
        P("ctx", "ch"),
        P("ctx", "ch"),
        P("ctx", "ch"),
    )
    return jax.shard_map(
        local,
        mesh=mesh,
        in_specs=placed,
        out_specs=(P(("ctx", "ch"), None), P("ctx", "ch")),
        check_vma=False,
    )
```

```python
import functools
import math

import jax
import jax.numpy as jnp
from jax import lax
from jax.experimental import pallas as pl
from jax.experimental.pallas import tpu as pltpu
from jax.sharding import PartitionSpec as P

STATE = 16
CONV = 4
HEADS = 64
KV_HEADS = 8
HEAD_DIM = 128


def halo(mamba_input, n_ctx, n_ch):
    width = mamba_input.shape[1] // n_ch
    tail = mamba_input[mamba_input.shape[0] - (CONV - 1) :]
    arrived = 0
    for j in range(n_ch):
        pairs = [(c * n_ch + n_ch - 1, (c + 1) * n_ch + j) for c in range(n_ctx - 1)]
        part = lax.ppermute(tail[:, j * width : (j + 1) * width], ("ctx", "ch"), pairs)
        arrived = arrived + part
    return arrived


LANES = 128
SUBS = 8
TILE = LANES * SUBS
LOG2E = math.log2(math.e)
MESH = pl.DeviceIdType.MESH


def to_rows(dst_ref, value):
    rows = value.shape[0]
    for sub in range(SUBS):
        dst_ref[pl.ds(sub, rows, stride=SUBS), :] = value[:, sub * LANES : (sub + 1) * LANES]


def spread_terms(terms_ref, spread_ref, count):
    rows = terms_ref.shape[0]
    for n in range(count):
        spread_ref[n * rows : (n + 1) * rows, :] = jnp.broadcast_to(
            terms_ref[:, n : n + 1], (rows, LANES)
        )


def row_of(spread_ref, index):
    return spread_ref[pl.ds(index, SUBS, stride=0), :]


PIECES = 4


def swap_copies(n_ch, src_ref, dst_ref, keep_sem, send_sem, recv_sem):
    me = lax.axis_index("ch")
    width = dst_ref.shape[2]
    piece = width // PIECES
    copies = []
    for p in range(PIECES):
        target = pl.ds(p * piece, piece)
        for k in range(1, n_ch):
            peer = lax.rem(me + k, n_ch)
            source = pl.ds(pl.multiple_of(peer * width + p * piece, LANES), piece)
            copies.append(pltpu.make_async_remote_copy(
                src_ref=src_ref.at[:, source], dst_ref=dst_ref.at[me, :, target],
                send_sem=send_sem.at[p, k], recv_sem=recv_sem.at[p, k],
                device_id={"ch": peer}, device_id_type=MESH))
    mine = pl.ds(pl.multiple_of(me * width, LANES), width)
    copies.append(pltpu.make_async_copy(src_ref.at[:, mine], dst_ref.at[me], keep_sem))
    return copies


def greet(axis, size):
    me = lax.axis_index(axis)
    for k in range(1, size):
        peer = lax.rem(me + k, size)
        pl.semaphore_signal(
            pltpu.get_barrier_semaphore(), inc=1, device_id={axis: peer}, device_id_type=MESH)


def first_pass(packing, low_ref, up_ref, bias_ref, act_ref, terms_ref, decay_ref,
               step_ref, packed_ref, spread, act_rows, rates, pack):
    rows = act_ref.shape[0]

    @pl.when(pl.program_id(0) == 0)
    def _():
        spread_terms(terms_ref, spread, STATE)

    pre = jnp.dot(low_ref[...], up_ref[...], preferred_element_type=jnp.float32) + bias_ref[...]
    to_rows(step_ref.at[0], jax.nn.softplus(pre))
    to_rows(act_rows, act_ref[...].astype(jnp.float32))
    to_rows(rates, decay_ref[...] * (-LOG2E))
    rate = [rates[n * SUBS : (n + 1) * SUBS, :] for n in range(STATE)]

    def token(t, carry):
        states, total = carry
        at = pl.multiple_of(t * SUBS, SUBS)
        step = step_ref[0, pl.ds(at, SUBS), :]
        push = step * act_rows[pl.ds(at, SUBS), :]
        states = tuple(
            jnp.exp2(step * rate[n]) * states[n] + push * row_of(spread, n * rows + t)
            for n in range(STATE)
        )
        return states, total + step

    zero = jnp.zeros((SUBS, LANES), jnp.float32)
    states, total = lax.fori_loop(0, rows, token, ((zero,) * STATE, zero), unroll=8)
    splits, subs, held, rows_state = packing
    total_hi = total.astype(jnp.bfloat16).astype(jnp.float32)
    pack[...] = jnp.zeros_like(pack)
    for part in range(pack.shape[0]):
        cut = slice(part // splits * subs, (part // splits + 1) * subs)
        for n in range(held):
            pack[part, n * subs : (n + 1) * subs] = states[part % splits * held + n][cut]
        pack[part, rows_state : rows_state + subs] = total_hi[cut]
        pack[part, rows_state + subs : rows_state + 2 * subs] = (total - total_hi)[cut]
    packed_ref[...] = pack[...].astype(jnp.bfloat16)


def second_pass(packing, n_ch, step_ref, act_ref, terms_ref, decay_ref, incoming_ref, skip_ref,
                out_ref, spread, act_rows, rates, outs, entering, wide, outbox,
                keep_sem, send_sem, recv_sem):
    rows = act_ref.shape[0]
    splits, subs, held, rows_state = packing
    tile, tiles = pl.program_id(0), pl.num_programs(0)
    me = lax.axis_index("ch")
    here = outbox.shape[1]
    channels = outbox.shape[2]

    @pl.when(tile == 0)
    def _():
        barrier = pltpu.get_barrier_semaphore()
        for k in range(1, n_ch):
            peer = lax.rem(me + k, n_ch)
            pl.semaphore_signal(barrier, inc=1, device_id={"ch": peer}, device_id_type=MESH)
        pl.semaphore_wait(barrier, n_ch - 1)
        spread_terms(terms_ref, spread, 2 * STATE)

    to_rows(act_rows, act_ref[...].astype(jnp.float32))
    to_rows(rates, decay_ref[...] * (-LOG2E))
    rate = [rates[n * SUBS : (n + 1) * SUBS, :] for n in range(STATE)]

    def token(t, states):
        at = pl.multiple_of(t * SUBS, SUBS)
        step = step_ref[0, pl.ds(at, SUBS), :]
        push = step * act_rows[pl.ds(at, SUBS), :]
        new, parts = [], []
        for n in range(STATE):
            state = jnp.exp2(step * rate[n]) * states[n] + push * row_of(spread, n * rows + t)
            new.append(state)
            term = state * row_of(spread, (STATE + n) * rows + t)
            if n < 2:
                parts.append(term)
            else:
                parts[n % 2] = parts[n % 2] + term
        outs[pl.ds(at, SUBS), :] = parts[0] + parts[1]
        return tuple(new)

    wide[...] = incoming_ref[...].astype(jnp.float32)
    for part in range(wide.shape[0]):
        for n in range(held):
            row = (part % splits * held + n) * SUBS + part // splits * subs
            entering[row : row + subs, :] = wide[part, n * subs : (n + 1) * subs]
    start = tuple(entering[n * SUBS : (n + 1) * SUBS, :] for n in range(STATE))
    lax.fori_loop(0, rows, token, start, unroll=8)
    first = pl.multiple_of(tile * TILE, TILE)
    for sub in range(SUBS):
        cols = slice(sub * LANES, (sub + 1) * LANES)
        mixed = outs[pl.ds(sub, rows, stride=SUBS), :]
        mixed = mixed + skip_ref[:, cols] * act_ref[:, cols].astype(jnp.float32)
        mixed = mixed.astype(jnp.bfloat16)
        at = pl.multiple_of(first + sub * LANES, LANES)
        for j in range(n_ch):
            outbox[j, :, pl.ds(at, LANES)] = mixed[j * here : (j + 1) * here]

    def keep(i):
        source = pl.multiple_of(i * TILE, TILE)
        target = pl.multiple_of(me * channels + i * TILE, TILE)
        return pltpu.make_async_copy(
            outbox.at[me, :, pl.ds(source, TILE)], out_ref.at[:, pl.ds(target, TILE)],
            keep_sem.at[i])

    def send(i, k):
        peer = lax.rem(me + k, n_ch)
        source = pl.multiple_of(i * TILE, TILE)
        target = pl.multiple_of(me * channels + i * TILE, TILE)
        return pltpu.make_async_remote_copy(
            src_ref=outbox.at[peer, :, pl.ds(source, TILE)],
            dst_ref=out_ref.at[:, pl.ds(target, TILE)],
            send_sem=send_sem.at[i, k], recv_sem=recv_sem.at[i, k],
            device_id={"ch": peer}, device_id_type=MESH)

    for k in range(1, n_ch):
        send(tile, k).start()
    keep(tile).start()

    @pl.when(tile == tiles - 1)
    def _():
        @pl.loop(0, tiles)
        def _(i):
            for k in range(1, n_ch):
                send(i, k).wait()
            keep(i).wait()


def swap_input(n_ch, src_ref, dst_ref, keep_sem, send_sem, recv_sem):
    greet("ch", n_ch)
    pl.semaphore_wait(pltpu.get_barrier_semaphore(), n_ch - 1)
    copies = swap_copies(n_ch, src_ref, dst_ref, keep_sem, send_sem, recv_sem)
    for copy in copies:
        copy.start()
    for copy in copies:
        copy.wait()


def exchange(n_ctx, rows_state, rows_total, send_ref, rate_ref, q_ref, kv_ref,
             back_ref, mixed_ref, got, reply, send_sem, got_sem, reply_sem, back_sem):
    me = lax.axis_index("ctx")
    rows = q_ref.shape[0]
    groups = kv_ref.shape[1] // 2 // HEAD_DIM
    block = q_ref.shape[1] // groups

    def attend(g, carry):
        k_at = pl.ds(pl.multiple_of(g * HEAD_DIM, HEAD_DIM), HEAD_DIM)
        v_at = pl.ds(pl.multiple_of((groups + g) * HEAD_DIM, HEAD_DIM), HEAD_DIM)
        first = pl.multiple_of(g * block, HEAD_DIM)
        parts = attend_group(
            me * rows, rows, q_ref[:, pl.ds(first, block)], kv_ref[:, k_at], kv_ref[:, v_at])
        for h, part in enumerate(parts):
            mixed_ref[:, pl.ds(pl.multiple_of(first + h * HEAD_DIM, HEAD_DIM), HEAD_DIM)] = part
        return carry

    greet("ctx", n_ctx)
    pl.semaphore_wait(pltpu.get_barrier_semaphore(), n_ctx - 1)

    def there(k):
        peer = lax.rem(me + k, n_ctx)
        return pltpu.make_async_remote_copy(
            src_ref=send_ref.at[peer], dst_ref=got.at[me], send_sem=send_sem.at[k],
            recv_sem=got_sem.at[k], device_id={"ctx": peer}, device_id_type=MESH)

    def back(k):
        peer = lax.rem(me + k, n_ctx)
        return pltpu.make_async_remote_copy(
            src_ref=reply.at[peer], dst_ref=back_ref.at[me], send_sem=reply_sem.at[k],
            recv_sem=back_sem.at[k], device_id={"ctx": peer}, device_id_type=MESH)

    for k in range(1, n_ctx):
        there(k).start()
    got[me] = send_ref[me]
    half = (groups + 1) // 2
    lax.fori_loop(0, half, attend, 0)
    for k in range(1, n_ctx):
        there(k).wait()

    state_shape = (rows_state, LANES)
    reps = rows_state // rows_total

    def combine(i, carry):
        sent = carry
        if reply.shape[1] > rows_state:
            spare = jnp.zeros((reply.shape[1] - rows_state, LANES), jnp.float32)
            sent = jnp.concatenate([carry, spare], axis=0)
        reply[i] = sent.astype(jnp.bfloat16)
        block = got[i].astype(jnp.float32)
        total = (block[rows_state : rows_state + rows_total]
                 + block[rows_state + rows_total : rows_state + 2 * rows_total])
        wide = jnp.concatenate([total] * reps, axis=0)
        return jnp.exp2(rate_ref[...] * wide) * carry + block[:rows_state]

    lax.fori_loop(0, n_ctx, combine, jnp.zeros(state_shape, jnp.float32))
    for k in range(1, n_ctx):
        back(k).start()
    back_ref[me] = reply[me]
    lax.fori_loop(half, groups, attend, 0)
    for k in range(1, n_ctx):
        back(k).wait()


def attend_group(query_first, rows, q, k, v):
    heads = q.shape[1] // HEAD_DIM
    stacked = jnp.concatenate(
        [q[:, h * HEAD_DIM : (h + 1) * HEAD_DIM] for h in range(heads)], axis=0
    )
    scores = lax.dot_general(
        stacked, k, (((1,), (1,)), ((), ())), preferred_element_type=jnp.float32
    ) * (LOG2E / math.sqrt(HEAD_DIM))
    query_pos = query_first + lax.broadcasted_iota(jnp.int32, scores.shape, 0) % rows
    visible = lax.broadcasted_iota(jnp.int32, scores.shape, 1) <= query_pos
    masked = jnp.where(visible, scores, -1e30)
    weights = jnp.exp2(masked - jnp.max(masked, axis=1, keepdims=True))
    total = jnp.sum(weights, axis=1, keepdims=True)
    mixed = jnp.dot(weights.astype(jnp.bfloat16), v, preferred_element_type=jnp.float32) / total
    mixed = mixed.astype(jnp.bfloat16)
    return [mixed[h * rows : (h + 1) * rows] for h in range(heads)]


def local(
    mamba_input, mamba_gate, conv_weight, conv_bias, step_down, state_proj, step_up, step_bias,
    decay_rate, skip_gain, queries, key_rows, value_rows,
):
    n_ctx, n_ch = lax.axis_size("ctx"), lax.axis_size("ch")
    kv = lax.all_gather(
        jnp.concatenate([key_rows, value_rows], axis=1), "ctx", axis=0, tiled=True)
    here, channels = mamba_input.shape[0], mamba_input.shape[1] // n_ch
    rows = here * n_ch
    limit = 56 * 1024 * 1024
    hbm = pl.BlockSpec(memory_space=pl.ANY)
    swapped = jax.ShapeDtypeStruct((n_ch, here, channels), jnp.bfloat16)
    swap_sems = [pltpu.SemaphoreType.DMA, pltpu.SemaphoreType.DMA((PIECES, n_ch)),
                 pltpu.SemaphoreType.DMA((PIECES, n_ch))]
    inner_in = pl.pallas_call(
        functools.partial(swap_input, n_ch),
        in_specs=[hbm],
        out_specs=hbm,
        out_shape=swapped,
        scratch_shapes=swap_sems,
        compiler_params=pltpu.CompilerParams(collective_id=2, has_side_effects=True),
        name="swap_input",
    )(mamba_input).reshape(rows, channels)
    rim_rows = halo(mamba_input, n_ctx, n_ch)
    padded = jnp.concatenate([rim_rows, inner_in], axis=0).astype(jnp.float32)
    conv_sum = conv_bias[None, :] + sum(
        conv_weight[tap][None, :] * padded[tap : tap + rows] for tap in range(CONV)
    )
    activation = jax.nn.silu(conv_sum).astype(jnp.bfloat16)
    low_part = jnp.dot(activation, step_down, preferred_element_type=jnp.float32)
    term_part = jnp.dot(activation, state_proj, preferred_element_type=jnp.float32)
    part = jnp.concatenate([low_part, term_part], axis=1)
    part_b = part.astype(jnp.bfloat16)
    summed = part
    for by in range(1, n_ch):
        pairs = [(i, (i + by) % n_ch) for i in range(n_ch)]
        summed = summed + lax.ppermute(part_b, "ch", pairs).astype(jnp.float32)
    rank = step_down.shape[1]
    step_low = summed[:, :rank].astype(jnp.bfloat16)
    state_terms = summed[:, rank:]

    tiles = channels // TILE
    f32, bf16 = jnp.float32, jnp.bfloat16
    whole = lambda shape: pl.BlockSpec(shape, lambda i: (0,) * len(shape))
    cols = lambda r: pl.BlockSpec((r, TILE), lambda i: (0, i))
    step_spec = pl.BlockSpec((1, rows * SUBS, LANES), lambda i: (i, 0, 0))
    tile_rows = rows * SUBS
    splits = max(1, n_ctx * LANES // channels)
    groups, held = n_ctx // splits, STATE // splits
    chunk = channels // groups
    subs = chunk // LANES
    parts = n_ctx // tiles
    rows_state = held * subs
    rows_back = -(-rows_state // 16) * 16
    rows_all = -(-(rows_state + 2 * subs) // 16) * 16
    packing = (splits, subs, held, rows_state)
    step_rows, packed = pl.pallas_call(
        functools.partial(first_pass, packing),
        grid=(tiles,),
        in_specs=[whole((rows, rank)), cols(rank), cols(1), cols(rows), whole((rows, 2 * STATE)),
                  cols(STATE)],
        out_specs=[step_spec, pl.BlockSpec((parts, rows_all, LANES), lambda i: (i, 0, 0))],
        out_shape=[
            jax.ShapeDtypeStruct((tiles, tile_rows, LANES), f32),
            jax.ShapeDtypeStruct((n_ctx, rows_all, LANES), bf16),
        ],
        scratch_shapes=[
            pltpu.VMEM((STATE * rows, LANES), f32),
            pltpu.VMEM((tile_rows, LANES), f32),
            pltpu.VMEM((STATE * SUBS, LANES), f32),
            pltpu.VMEM((parts, rows_all, LANES), f32),
        ],
        compiler_params=pltpu.CompilerParams(vmem_limit_bytes=limit),
        name="first_pass",
    )(step_low, step_up, step_bias[None], activation, state_terms, decay_rate)

    me = lax.axis_index("ctx")
    my_rate = lax.dynamic_slice(
        decay_rate, (me % splits * held, me // splits * chunk), (held, chunk))
    my_rate = (my_rate * (-LOG2E)).reshape(rows_state, LANES)
    vmem = pl.BlockSpec(memory_space=pltpu.VMEM)
    incoming, attention_out = pl.pallas_call(
        functools.partial(exchange, n_ctx, rows_state, subs),
        in_specs=[vmem] * 4,
        out_specs=[vmem] * 2,
        out_shape=[
            jax.ShapeDtypeStruct((n_ctx, rows_back, LANES), bf16),
            jax.ShapeDtypeStruct(queries.shape, bf16),
        ],
        scratch_shapes=[
            pltpu.VMEM((n_ctx, rows_all, LANES), bf16),
            pltpu.VMEM((n_ctx, rows_back, LANES), bf16),
        ] + [pltpu.SemaphoreType.DMA((n_ctx,))] * 4,
        compiler_params=pltpu.CompilerParams(
            collective_id=0, has_side_effects=True, vmem_limit_bytes=limit),
        name="exchange",
    )(packed, my_rate, queries, kv)

    scan_out = pl.pallas_call(
        functools.partial(second_pass, packing, n_ch),
        grid=(tiles,),
        in_specs=[
            step_spec, cols(rows), whole((rows, 2 * STATE)), cols(STATE),
            pl.BlockSpec((parts, rows_back, LANES), lambda i: (i, 0, 0)),
            cols(1),
        ],
        out_specs=pl.BlockSpec(memory_space=pl.ANY),
        out_shape=jax.ShapeDtypeStruct(mamba_input.shape, bf16),
        scratch_shapes=[
            pltpu.VMEM((2 * STATE * rows, LANES), f32),
            pltpu.VMEM((tile_rows, LANES), f32),
            pltpu.VMEM((STATE * SUBS, LANES), f32),
            pltpu.VMEM((tile_rows, LANES), f32),
            pltpu.VMEM((STATE * SUBS, LANES), f32),
            pltpu.VMEM((parts, rows_back, LANES), f32),
            pltpu.VMEM((n_ch, rows // n_ch, channels), bf16),
            pltpu.SemaphoreType.DMA((tiles,)),
            pltpu.SemaphoreType.DMA((tiles, n_ch)),
            pltpu.SemaphoreType.DMA((tiles, n_ch)),
        ],
        compiler_params=pltpu.CompilerParams(
            collective_id=1, has_side_effects=True, vmem_limit_bytes=limit),
        name="second_pass",
    )(step_rows, activation, state_terms, decay_rate, incoming,
      skip_gain[None])
    mamba_out = (scan_out.astype(f32) * jax.nn.silu(mamba_gate.astype(f32))).astype(bf16)
    return (mamba_out, attention_out)


def solution(mesh):
    placed = (
        P(("ctx", "ch"), None),
        P(("ctx", "ch"), None),
        P(None, "ch"),
        P("ch"),
        P("ch", None),
        P("ch", None),
        P(None, "ch"),
        P("ch"),
        P(None, "ch"),
        P("ch"),
        P("ctx", "ch"),
        P("ctx", "ch"),
        P("ctx", "ch"),
    )
    return jax.shard_map(
        local,
        mesh=mesh,
        in_specs=placed,
        out_specs=(P(("ctx", "ch"), None), P("ctx", "ch")),
        check_vma=False,
    )
```
